32 devices in a mesh: ia: 4 (over y, x), ja: 8 (over z, core), ka: 1.
Axes of the slice: x: 2, y: 2, z: 4, core: 2. Of those that a mesh axis runs over, the one named last changes fastest.
Arguments:
- tensor: bfloat16 [8, 2048, 4096], P('ka', 'ia', 'ja'), may hold values from -6 to 6
- factor_b: float32 [32, 4096], P('ia', ('ja', 'ka')), may hold values from -0.09375 to 0.09375
- factor_c: float32 [32, 8], P(('ia', 'ja'), 'ka'), may hold values from -2 to 2
Outputs:
- factor_a_new: float32 [32, 2048], P('ja', ('ia', 'ka'))
- factor_b_new: float32 [32, 4096], P('ia', ('ja', 'ka'))
The draws below stay inside these ranges and needn't reach their ends.
All inputs are finite; a program needn't handle non-finite values.
Results may differ from the reference program's by a relative error of at most 0.0033.
Values sent between devices are 32-bit elements; how exact they have to be, the bound alone decides.
A program may use at most 64 MiB of HBM per device.

```python
import jax
import jax.numpy as jnp
from jax import lax

R = 32
I = 2048
J = 4096
K = 8


def block_levels(key, dims, pieces, least, top_value):
    def one(position, parts):
        draws = jax.random.uniform(jax.random.fold_in(jax.random.fold_in(key, 6), position), (parts,), jnp.float32, least / len(pieces), top_value / len(pieces))
        return jnp.repeat(jnp.exp(draws), dims[position] // parts).reshape((-1,) + (1,) * (len(dims) - position - 1))

    level = one(*pieces[0])
    for cut in pieces[1:]:
        level = level * one(*cut)
    return level


def gaussian(stream_key, extent, width, bound, cuts=(), dtype=jnp.bfloat16):
    entries = width * jax.random.normal(stream_key, extent, jnp.float32)
    if cuts:
        entries = entries * block_levels(stream_key, extent, cuts, -0.22, 0.18)
    return jnp.clip(entries, -bound, bound).astype(dtype)


def setup_inputs(seed: int = 0) -> dict:
    arg_keys = jax.random.split(jax.random.key(seed), 4)
    tensor = gaussian(arg_keys[0], (K, I, J), 1.0, 6.0, ((1, 4), (2, 8)))
    factor_b = gaussian(arg_keys[1], (R, J), J ** -0.5, 0.09375, ((0, 4), (1, 8)), jnp.float32)
    factor_c = gaussian(arg_keys[2], (R, K), K ** -0.5, 2.0, ((0, 32),), jnp.float32)
    return {"tensor": tensor, "factor_b": factor_b, "factor_c": factor_c}


EPS = 1e-06
HIGH = lax.Precision.HIGHEST

def gram_of(block):
    return jnp.dot(block.astype(jnp.float32), block.T.astype(jnp.float32), precision=HIGH, preferred_element_type=jnp.float32)

def solve_with(normal, rhs):
    lower = jnp.linalg.cholesky(normal)
    return jax.scipy.linalg.cho_solve((lower, True), rhs)

def unit_rows(raw):
    mean_square = lax.optimization_barrier(jnp.mean(raw * raw, axis=1))
    return raw / jnp.sqrt(mean_square + EPS)[:, None]

def reference(tensor, factor_b, factor_c):
    gram_b = gram_of(factor_b)
    gram_c = gram_of(factor_c)
    normal_a = gram_b * gram_c
    columns_c = factor_c.T

    def step_a(total, item):
        slab, weights = item
        kr_slab = (weights[:, None] * factor_b).astype(jnp.bfloat16)
        return (total + jnp.dot(kr_slab.astype(jnp.float32), slab.T.astype(jnp.float32), preferred_element_type=jnp.float32), None)
    start_a = jnp.zeros((factor_b.shape[0], tensor.shape[1]), jnp.float32)
    mttkrp_a, _ = lax.scan(step_a, start_a, (tensor, columns_c))
    factor_a_new = unit_rows(solve_with(normal_a, mttkrp_a))
    normal_b = gram_of(factor_a_new) * gram_c

    def step_b(total, item):
        slab, weights = item
        kr_slab = (weights[:, None] * factor_a_new).astype(jnp.bfloat16)
        return (total + jnp.dot(kr_slab.astype(jnp.float32), slab.astype(jnp.float32), preferred_element_type=jnp.float32), None)
    start_b = jnp.zeros((factor_b.shape[0], tensor.shape[2]), jnp.float32)
    mttkrp_b, _ = lax.scan(step_b, start_b, (tensor, columns_c))
    factor_b_new = unit_rows(solve_with(normal_b, mttkrp_b))
    return (factor_a_new, factor_b_new)
```

```python
import functools

import jax
import jax.numpy as jnp
from jax import lax
from jax.experimental import pallas as pl
from jax.experimental.pallas import tpu as pltpu
from jax.sharding import PartitionSpec as P

EPS = 1e-06
HIGH = lax.Precision.HIGHEST


def gram_of(block):
    return jnp.dot(block, block.T, precision=HIGH, preferred_element_type=jnp.float32)


def solve_with(normal, rhs):
    lower = jnp.linalg.cholesky(normal)
    return jax.scipy.linalg.cho_solve((lower, True), rhs)


def arrange(partial_rows, rows_split, cols_split):
    rank, width = partial_rows.shape
    grid = partial_rows.reshape(rows_split, rank // rows_split, cols_split, width // cols_split)
    return grid.transpose(0, 2, 1, 3).reshape(rank * cols_split, width // cols_split)


def assemble(pieces, rows_split, cols_split):
    count, height, width = pieces.shape
    grid = pieces.reshape(rows_split, cols_split, height, width)
    return grid.transpose(0, 2, 1, 3).reshape(rows_split * height, cols_split * width)


def scaled(raw, squares, total):
    return raw / jnp.sqrt(squares / total + EPS)[:, None]


def body(tensor, factor_b, factor_c):
    n_ia = lax.axis_size("ia")
    n_ja = lax.axis_size("ja")
    n_ka = lax.axis_size("ka")
    total_i = tensor.shape[1] * n_ia
    total_j = tensor.shape[2] * n_ja
    c_block = lax.all_gather(factor_c, ("ia", "ja"), axis=0, tiled=True)
    pieces = lax.all_gather(factor_b[None], ("ia", "ka"), axis=0, tiled=True)
    b_block = assemble(pieces, n_ia, n_ka)
    gram_b = lax.psum(gram_of(b_block), "ja")
    gram_c = lax.psum(gram_of(c_block), "ka")
    normal_a = gram_b * gram_c
    kr_a = (c_block[:, :, None] * b_block[:, None, :]).astype(jnp.bfloat16)
    partial_a = jnp.einsum("rkj,kij->ri", kr_a, tensor, preferred_element_type=jnp.float32)
    solved_a = solve_with(normal_a, partial_a)
    raw_a = lax.psum_scatter(
        arrange(solved_a, n_ja, n_ka), ("ja", "ka"), scatter_dimension=0, tiled=True
    )
    squares_a = lax.psum(jnp.sum(raw_a * raw_a, axis=1), ("ia", "ka"))
    local_a = scaled(raw_a, squares_a, total_i)
    pieces_a = lax.all_gather(local_a[None], ("ja", "ka"), axis=0, tiled=True)
    gathered_a = assemble(pieces_a, n_ja, n_ka)
    gram_a = lax.psum(gram_of(gathered_a), "ia")
    normal_b = gram_a * gram_c
    kr_b = (c_block[:, :, None] * gathered_a[:, None, :]).astype(jnp.bfloat16)
    partial_b = jnp.einsum("rki,kij->rj", kr_b, tensor, preferred_element_type=jnp.float32)
    solved_b = solve_with(normal_b, partial_b)
    raw_b = lax.psum_scatter(
        arrange(solved_b, n_ia, n_ka), ("ia", "ka"), scatter_dimension=0, tiled=True
    )
    squares_b = lax.psum(jnp.sum(raw_b * raw_b, axis=1), ("ja", "ka"))
    share_b = scaled(raw_b, squares_b, total_j)
    return (local_a, share_b)


MESH = pl.DeviceIdType.MESH
LANES = 128
SUBS = 8
NT = (((1,), (1,)), ((), ()))


def spread(src, dst, me, count, device, send, recv):
    copies = []
    for step in range(1, count):
        copies.append(
            pltpu.make_async_remote_copy(
                src_ref=src,
                dst_ref=dst.at[me],
                send_sem=send.at[step],
                recv_sem=recv.at[step],
                device_id=device(lax.rem(me + step, count)),
                device_id_type=MESH,
            )
        )
    return copies


def stacked(pieces, rows):
    height, width = sum(p.shape[0] for p in pieces), pieces[0].shape[1]
    if rows > height:
        pieces = list(pieces) + [jnp.zeros((rows - height, width), pieces[0].dtype)]
    return jnp.concatenate(pieces, axis=0)


def wide_gram(block):
    other = stacked([block], LANES)
    return lax.dot_general(block, other, NT, precision=HIGH, preferred_element_type=jnp.float32)


def packed(gram):
    rank = gram.shape[0]
    tile = gram[0:SUBS]
    for q in range(1, rank // SUBS):
        tile = tile + pltpu.roll(gram[q * SUBS : (q + 1) * SUBS], q * rank, 1)
    return tile


def unpacked(tile, rank):
    lane = lax.broadcasted_iota(jnp.int32, (SUBS, LANES), 1)
    groups = []
    for q in range(rank // SUBS):
        moved = tile if q == 0 else pltpu.roll(tile, LANES - q * rank, 1)
        groups.append(jnp.where(lane < rank, moved, 0.0))
    return jnp.concatenate(groups, axis=0)


def inverse(normal):
    rank = normal.shape[0]
    lane = lax.broadcasted_iota(jnp.int32, normal.shape, 1)
    sub = lax.broadcasted_iota(jnp.int32, normal.shape, 0)
    for k in range(rank):
        col = normal[:, k : k + 1]
        row = normal[k : k + 1, :]
        pivot = 1.0 / normal[k : k + 1, k : k + 1]
        row = jnp.where(lane[0:1] == k, 1.0, row) * pivot
        rest = jnp.where(lane == k, 0.0, normal) - col * row
        normal = jnp.where(sub == k, row, rest)
    return normal


def split(values):
    high = values.astype(jnp.bfloat16).astype(jnp.float32)
    return high, values - high


def kernel(
    n_ia, n_ja, total_i, total_j,
    t_ref, b_ref, c_ref, oa_ref, ob_ref,
    tv, ball, cst, cja, cia, gb, pbuf, ra, ga, araw, gr, rb, wsc, sq,
    t_sem, b_s, b_r, cj_s, cj_r, ci_s, ci_r, gb_s, gb_r, ra_s, ra_r, ga_s, ga_r,
    gr_s, gr_r, rb_s, rb_r, sq_s, sq_r,
):
    a = lax.axis_index("ia")
    j = lax.axis_index("ja")
    steps, width_i, width_j = tv.shape
    rank = n_ia * b_ref.shape[0]
    groups = rank // SUBS
    halves = n_ja // groups
    part_i = width_i // halves
    cuts_j = rb.shape[0]
    part_j = width_j // cuts_j

    def on_ia(index):
        return (index, j, 0)

    def on_ja(index):
        return (a, index, 0)

    loads = []
    for h in range(halves):
        rows = pl.ds(h * part_i, part_i)
        load = pltpu.make_async_copy(t_ref.at[:, rows], tv.at[:, rows], t_sem.at[h])
        load.start()
        loads.append(load)

    barrier = pltpu.get_barrier_semaphore()
    for step in range(1, n_ia):
        pl.semaphore_signal(barrier, inc=1, device_id=on_ia(lax.rem(a + step, n_ia)), device_id_type=MESH)
    for step in range(1, n_ja):
        pl.semaphore_signal(barrier, inc=1, device_id=on_ja(lax.rem(j + step, n_ja)), device_id_type=MESH)
    cst[...] = jnp.zeros_like(cst)
    cst[0:1, 0:steps] = c_ref[...]
    cja[j] = cst[...]
    ball[a] = b_ref[...]
    pl.semaphore_wait(barrier, n_ia + n_ja - 2)

    sends = []

    def begin(copies):
        for copy in copies:
            copy.start()
        sends.extend(copies)
        return copies

    def arrived(copies):
        for copy in copies:
            copy.wait_recv()

    b_copies = begin(spread(b_ref, ball, a, n_ia, on_ia, b_s, b_r))
    cj_copies = begin(spread(cst, cja, j, n_ja, on_ja, cj_s, cj_r))
    arrived(cj_copies)
    cia[a] = stacked([cja[s, 0:1, :] for s in range(n_ja)], n_ja)
    ci_copies = begin(spread(cia.at[a], cia, a, n_ia, on_ia, ci_s, ci_r))
    arrived(b_copies)
    b_all = stacked([ball[s] for s in range(n_ia)], rank)
    gb[j] = packed(wide_gram(b_all))
    gb_copies = begin(spread(gb.at[j], gb, j, n_ja, on_ja, gb_s, gb_r))
    weights = stacked(list(split(b_all)), LANES).T.astype(jnp.bfloat16)
    arrived(ci_copies)
    c_all = stacked([cia[s] for s in range(n_ia)], rank)
    gram_c = wide_gram(c_all)
    c_rows = stacked([c_all, c_all], LANES).T

    ra_copies = []
    for step in range(1, n_ja):
        peer = lax.rem(j + step, n_ja)
        ra_copies.append(
            pltpu.make_async_remote_copy(
                src_ref=pbuf.at[peer],
                dst_ref=ra.at[j],
                send_sem=ra_s.at[step],
                recv_sem=ra_r.at[step],
                device_id=on_ja(peer),
                device_id_type=MESH,
            )
        )
    for h in range(halves):
        loads[h].wait()
        total = jnp.zeros((part_i, LANES), jnp.float32)
        for k in range(steps):
            product = jnp.dot(
                tv[k, h * part_i : (h + 1) * part_i, :], weights, preferred_element_type=jnp.float32
            )
            total = total + product * c_rows[k : k + 1, :]
        total = total.T
        total = total[0:rank] + total[rank : 2 * rank]
        for q in range(groups):
            pbuf[q * halves + h] = total[q * SUBS : (q + 1) * SUBS]
        for step in range(1, n_ja):
            @pl.when(lax.rem(j + step, halves) == h)
            def _():
                ra_copies[step - 1].start()
    sends.extend(ra_copies)
    ra[j] = pbuf[j]

    arrived(gb_copies)
    gram_b = unpacked(functools.reduce(jnp.add, [gb[s] for s in range(n_ja)]), rank)
    solve_a = inverse(gram_b * gram_c)

    arrived(ra_copies)
    ga[j] = functools.reduce(jnp.add, [ra[s] for s in range(n_ja)])
    ga_copies = begin(spread(ga.at[j], ga, j, n_ja, on_ja, ga_s, ga_r))
    c_cols = [c_all[:, k : k + 1] for k in range(steps)]
    arrived(ga_copies)
    summed = stacked(
        [
            jnp.concatenate([ga[q * halves + h] for h in range(halves)], axis=1)
            for q in range(groups)
        ],
        rank,
    )
    raw_a = jnp.dot(solve_a[:, 0:rank], summed, precision=HIGH, preferred_element_type=jnp.float32)
    araw[...] = raw_a
    gr[a] = packed(wide_gram(raw_a))
    gr_copies = begin(spread(gr.at[a], gr, a, n_ia, on_ia, gr_s, gr_r))

    rb_copies = []
    pieces = []
    for k in range(steps):
        pieces.append(jnp.concatenate(split(raw_a * c_cols[k]), axis=0).astype(jnp.bfloat16))
    for h in range(cuts_j):
        total = jnp.zeros((2 * rank, part_j), jnp.float32)
        for k in range(steps):
            total = total + jnp.dot(
                pieces[k], tv[k, :, h * part_j : (h + 1) * part_j], preferred_element_type=jnp.float32
            )
        rb[h, a] = total[0:rank] + total[rank : 2 * rank]
        rb_copies.extend(
            begin(spread(rb.at[h, a], rb.at[h], a, n_ia, on_ia, rb_s.at[h], rb_r.at[h]))
        )

    arrived(gr_copies)
    gram_a = unpacked(functools.reduce(jnp.add, [gr[s] for s in range(n_ia)]), rank)
    lane = lax.broadcasted_iota(jnp.int32, (rank, LANES), 1)
    sub = lax.broadcasted_iota(jnp.int32, (rank, LANES), 0)
    squares = jnp.where(lane == sub, gram_a, 0.0)
    scale_col = 1.0 / jnp.sqrt(jnp.sum(squares, axis=1, keepdims=True) / total_i + EPS)
    scale_row = 1.0 / jnp.sqrt(jnp.sum(squares, axis=0, keepdims=True) / total_i + EPS)
    solve_b = inverse(gram_a * scale_col * scale_row * gram_c) * scale_row
    for q in range(n_ia):
        wsc[q] = solve_b[q * SUBS : (q + 1) * SUBS]
    new_a = araw[...] * scale_col
    for q in range(groups):
        araw[q * SUBS : (q + 1) * SUBS] = new_a[q * SUBS : (q + 1) * SUBS]
    height = rank // n_ja
    for p in range(n_ja):
        @pl.when(j == p)
        def _():
            oa_ref[...] = araw[p * height : (p + 1) * height, :]
    solve_own = wsc[a][:, 0:rank]

    arrived(rb_copies)
    raw_b = []
    for h in range(cuts_j):
        summed_b = functools.reduce(jnp.add, [rb[h, s] for s in range(n_ia)])
        raw_b.append(
            jnp.dot(solve_own, summed_b, precision=HIGH, preferred_element_type=jnp.float32)
        )
    raw_b = jnp.concatenate(raw_b, axis=1)
    sq[j] = jnp.broadcast_to(jnp.sum(raw_b * raw_b, axis=1, keepdims=True), (SUBS, LANES))
    sq_copies = begin(spread(sq.at[j], sq, j, n_ja, on_ja, sq_s, sq_r))
    arrived(sq_copies)
    squares_b = functools.reduce(jnp.add, [sq[s] for s in range(n_ja)])[:, 0:1]
    ob_ref[...] = raw_b / jnp.sqrt(squares_b / total_j + EPS)

    for copy in sends:
        copy.wait_send()


def fused(tensor, factor_b, factor_c):
    n_ia = lax.axis_size("ia")
    n_ja = lax.axis_size("ja")
    steps, width_i, width_j = tensor.shape
    rows_b = factor_b.shape[0]
    rank = rows_b * n_ia
    halves = n_ja // (rank // SUBS)
    cuts_j = 2
    f32 = jnp.float32
    vmem = pltpu.VMEM
    dma = pltpu.SemaphoreType.DMA
    ja_sems = [dma((n_ja,)), dma((n_ja,))]
    ia_sems = [dma((n_ia,)), dma((n_ia,))]
    scratch = [
        vmem(tensor.shape, tensor.dtype),
        vmem((n_ia, rows_b, width_j), f32),
        vmem((SUBS, LANES), f32),
        vmem((n_ja, SUBS, LANES), f32),
        vmem((n_ia, n_ja, LANES), f32),
        vmem((n_ja, SUBS, LANES), f32),
        vmem((n_ja, SUBS, width_i // halves), f32),
        vmem((n_ja, SUBS, width_i // halves), f32),
        vmem((n_ja, SUBS, width_i // halves), f32),
        vmem((rank, width_i), f32),
        vmem((n_ia, SUBS, LANES), f32),
        vmem((cuts_j, n_ia, rank, width_j // cuts_j), f32),
        vmem((n_ia, SUBS, LANES), f32),
        vmem((n_ja, SUBS, LANES), f32),
        dma((halves,)),
        *ia_sems, *ja_sems, *ia_sems, *ja_sems, *ja_sems, *ja_sems, *ia_sems,
        dma((cuts_j, n_ia)), dma((cuts_j, n_ia)),
        *ja_sems,
    ]
    flops = 8 * rank * tensor.size
    return pl.pallas_call(
        functools.partial(kernel, n_ia, n_ja, width_i * n_ia, width_j * n_ja),
        out_shape=(
            jax.ShapeDtypeStruct((rank // n_ja, width_i), f32),
            jax.ShapeDtypeStruct((rows_b, width_j), f32),
        ),
        in_specs=[
            pl.BlockSpec(memory_space=pl.ANY),
            pl.BlockSpec(memory_space=pltpu.VMEM),
            pl.BlockSpec(memory_space=pltpu.VMEM),
        ],
        out_specs=(pl.BlockSpec(memory_space=pltpu.VMEM), pl.BlockSpec(memory_space=pltpu.VMEM)),
        scratch_shapes=scratch,
        cost_estimate=pl.CostEstimate(flops=flops, bytes_accessed=2 * tensor.size, transcendentals=0),
        compiler_params=pltpu.CompilerParams(
            collective_id=0, has_side_effects=True, vmem_limit_bytes=40 * 2**20
        ),
    )(tensor, factor_b, factor_c)


def fits(mesh):
    n_ia, n_ja, n_ka = (mesh.shape[name] for name in ("ia", "ja", "ka"))
    return n_ka == 1 and n_ia * SUBS == 32 and n_ja % n_ia == 0 and n_ja <= SUBS


def solution(mesh):
    return jax.shard_map(
        fused if fits(mesh) else body,
        mesh=mesh,
        in_specs=(P("ka", "ia", "ja"), P("ia", ("ja", "ka")), P(("ia", "ja"), "ka")),
        out_specs=(P("ja", ("ia", "ka")), P("ia", ("ja", "ka"))),
        check_vma=False,
    )
```

```python
import functools

import jax
import jax.numpy as jnp
from jax import lax
from jax.experimental import pallas as pl
from jax.experimental.pallas import tpu as pltpu
from jax.sharding import PartitionSpec as P

EPS = 1e-06
HIGH = lax.Precision.HIGHEST


def gram_of(block):
    return jnp.dot(block, block.T, precision=HIGH, preferred_element_type=jnp.float32)


def solve_with(normal, rhs):
    lower = jnp.linalg.cholesky(normal)
    return jax.scipy.linalg.cho_solve((lower, True), rhs)


def arrange(partial_rows, rows_split, cols_split):
    rank, width = partial_rows.shape
    grid = partial_rows.reshape(rows_split, rank // rows_split, cols_split, width // cols_split)
    return grid.transpose(0, 2, 1, 3).reshape(rank * cols_split, width // cols_split)


def assemble(pieces, rows_split, cols_split):
    count, height, width = pieces.shape
    grid = pieces.reshape(rows_split, cols_split, height, width)
    return grid.transpose(0, 2, 1, 3).reshape(rows_split * height, cols_split * width)


def scaled(raw, squares, total):
    return raw / jnp.sqrt(squares / total + EPS)[:, None]


def body(tensor, factor_b, factor_c):
    n_ia = lax.axis_size("ia")
    n_ja = lax.axis_size("ja")
    n_ka = lax.axis_size("ka")
    total_i = tensor.shape[1] * n_ia
    total_j = tensor.shape[2] * n_ja
    c_block = lax.all_gather(factor_c, ("ia", "ja"), axis=0, tiled=True)
    pieces = lax.all_gather(factor_b[None], ("ia", "ka"), axis=0, tiled=True)
    b_block = assemble(pieces, n_ia, n_ka)
    gram_b = lax.psum(gram_of(b_block), "ja")
    gram_c = lax.psum(gram_of(c_block), "ka")
    normal_a = gram_b * gram_c
    kr_a = (c_block[:, :, None] * b_block[:, None, :]).astype(jnp.bfloat16)
    partial_a = jnp.einsum("rkj,kij->ri", kr_a, tensor, preferred_element_type=jnp.float32)
    solved_a = solve_with(normal_a, partial_a)
    raw_a = lax.psum_scatter(
        arrange(solved_a, n_ja, n_ka), ("ja", "ka"), scatter_dimension=0, tiled=True
    )
    squares_a = lax.psum(jnp.sum(raw_a * raw_a, axis=1), ("ia", "ka"))
    local_a = scaled(raw_a, squares_a, total_i)
    pieces_a = lax.all_gather(local_a[None], ("ja", "ka"), axis=0, tiled=True)
    gathered_a = assemble(pieces_a, n_ja, n_ka)
    gram_a = lax.psum(gram_of(gathered_a), "ia")
    normal_b = gram_a * gram_c
    kr_b = (c_block[:, :, None] * gathered_a[:, None, :]).astype(jnp.bfloat16)
    partial_b = jnp.einsum("rki,kij->rj", kr_b, tensor, preferred_element_type=jnp.float32)
    solved_b = solve_with(normal_b, partial_b)
    raw_b = lax.psum_scatter(
        arrange(solved_b, n_ia, n_ka), ("ia", "ka"), scatter_dimension=0, tiled=True
    )
    squares_b = lax.psum(jnp.sum(raw_b * raw_b, axis=1), ("ja", "ka"))
    share_b = scaled(raw_b, squares_b, total_j)
    return (local_a, share_b)


MESH = pl.DeviceIdType.MESH
LANES = 128
SUBS = 8
NT = (((1,), (1,)), ((), ()))


def spread(src, dst, me, count, device, send, recv):
    copies = []
    for step in range(1, count):
        copies.append(
            pltpu.make_async_remote_copy(
                src_ref=src,
                dst_ref=dst.at[me],
                send_sem=send.at[step],
                recv_sem=recv.at[step],
                device_id=device(lax.rem(me + step, count)),
                device_id_type=MESH,
            )
        )
    return copies


def stacked(pieces, rows):
    height, width = sum(p.shape[0] for p in pieces), pieces[0].shape[1]
    if rows > height:
        pieces = list(pieces) + [jnp.zeros((rows - height, width), pieces[0].dtype)]
    return jnp.concatenate(pieces, axis=0)


def wide_gram(block):
    other = stacked([block], LANES)
    return lax.dot_general(block, other, NT, precision=HIGH, preferred_element_type=jnp.float32)


def packed(gram):
    rank = gram.shape[0]
    tile = gram[0:SUBS]
    for q in range(1, rank // SUBS):
        tile = tile + pltpu.roll(gram[q * SUBS : (q + 1) * SUBS], q * rank, 1)
    return tile


def unpacked(tile, rank):
    lane = lax.broadcasted_iota(jnp.int32, (SUBS, LANES), 1)
    groups = []
    for q in range(rank // SUBS):
        moved = tile if q == 0 else pltpu.roll(tile, LANES - q * rank, 1)
        groups.append(jnp.where(lane < rank, moved, 0.0))
    return jnp.concatenate(groups, axis=0)


def inverse(normal):
    rank = normal.shape[0]
    blocks = [normal[q * SUBS : (q + 1) * SUBS] for q in range(rank // SUBS)]
    lane = lax.broadcasted_iota(jnp.int32, (SUBS, LANES), 1)
    sub = lax.broadcasted_iota(jnp.int32, (SUBS, LANES), 0)

    def column(block, index):
        return jnp.broadcast_to(block[:, index : index + 1], (SUBS, LANES))

    for q in range(rank // SUBS):
        first = q * SUBS
        cols = [[column(block, first + k) for k in range(SUBS)] for block in blocks]
        rows, inner = blocks[q], cols[q]
        for k in range(SUBS):
            col = inner[k]
            pivot = 1.0 / col[k : k + 1]
            row = jnp.where(lane[0:1] == first + k, 1.0, rows[k : k + 1]) * pivot
            rest = jnp.where(lane == first + k, 0.0, rows) - col * row
            rows = jnp.where(sub == k, row, rest)
            for m in range(k + 1, SUBS):
                entry = inner[m][k : k + 1] * pivot
                inner[m] = jnp.where(sub == k, entry, inner[m] - col * entry)
        inside = (lane >= first) & (lane < first + SUBS)
        for p in range(rank // SUBS):
            if p != q:
                total = jnp.where(inside, 0.0, blocks[p])
                for k in range(SUBS):
                    total = total - cols[p][k] * rows[k : k + 1]
                blocks[p] = total
        blocks[q] = rows
    return jnp.concatenate(blocks, axis=0)


def split(values):
    high = values.astype(jnp.bfloat16).astype(jnp.float32)
    return high, values - high


def kernel(
    n_ia, n_ja, total_i, total_j,
    t_ref, b_ref, c_ref, oa_ref, ob_ref,
    tv, ball, cin, cst, cja, cia, gb, pbuf, ra, ga, araw, gr, rb, wsc, sq,
    t_sem, in_sem, b_s, b_r, cj_s, cj_r, ci_s, ci_r, gb_s, gb_r, ra_s, ra_r, ga_s, ga_r,
    gr_s, gr_r, rb_s, rb_r, sq_s, sq_r,
):
    a = lax.axis_index("ia")
    j = lax.axis_index("ja")
    steps, width_i, width_j = tv.shape
    rank = n_ia * b_ref.shape[0]
    groups = rank // SUBS
    halves = n_ja // groups
    part_i = width_i // halves
    cuts_j = rb.shape[0]
    part_j = width_j // cuts_j

    def on_ia(index):
        return (index, j, 0)

    def on_ja(index):
        return (a, index, 0)

    fetch_c = pltpu.make_async_copy(c_ref, cin, in_sem.at[0])
    fetch_b = pltpu.make_async_copy(b_ref, ball.at[a], in_sem.at[1])
    fetch_c.start()
    fetch_b.start()
    loads = []
    for h in range(halves):
        rows = pl.ds(h * part_i, part_i)
        load = pltpu.make_async_copy(t_ref.at[:, rows], tv.at[:, rows], t_sem.at[h])
        load.start()
        loads.append(load)

    barrier = pltpu.get_barrier_semaphore()
    for step in range(1, n_ia):
        pl.semaphore_signal(barrier, inc=1, device_id=on_ia(lax.rem(a + step, n_ia)), device_id_type=MESH)
    for step in range(1, n_ja):
        pl.semaphore_signal(barrier, inc=1, device_id=on_ja(lax.rem(j + step, n_ja)), device_id_type=MESH)
    cst[...] = jnp.zeros_like(cst)
    fetch_c.wait()
    cst[0:1, 0:steps] = cin[...]
    cja[j] = cst[...]
    fetch_b.wait()
    pl.semaphore_wait(barrier, n_ia + n_ja - 2)

    sends = []

    def begin(copies):
        for copy in copies:
            copy.start()
        sends.extend(copies)
        return copies

    def arrived(copies):
        for copy in copies:
            copy.wait_recv()

    b_copies = begin(spread(ball.at[a], ball, a, n_ia, on_ia, b_s, b_r))
    cj_copies = begin(spread(cst, cja, j, n_ja, on_ja, cj_s, cj_r))
    arrived(cj_copies)
    cia[a] = stacked([cja[s, 0:1, :] for s in range(n_ja)], n_ja)
    ci_copies = begin(spread(cia.at[a], cia, a, n_ia, on_ia, ci_s, ci_r))
    arrived(b_copies)
    b_all = stacked([ball[s] for s in range(n_ia)], rank)
    gb[j] = packed(wide_gram(b_all))
    gb_copies = begin(spread(gb.at[j], gb, j, n_ja, on_ja, gb_s, gb_r))
    weights = stacked(list(split(b_all)), LANES).T.astype(jnp.bfloat16)
    arrived(ci_copies)
    c_all = stacked([cia[s] for s in range(n_ia)], rank)
    gram_c = wide_gram(c_all)
    c_rows = stacked([c_all, c_all], LANES).T

    ra_copies = []
    for step in range(1, n_ja):
        peer = lax.rem(j + step, n_ja)
        ra_copies.append(
            pltpu.make_async_remote_copy(
                src_ref=pbuf.at[peer],
                dst_ref=ra.at[j],
                send_sem=ra_s.at[step],
                recv_sem=ra_r.at[step],
                device_id=on_ja(peer),
                device_id_type=MESH,
            )
        )
    for h in range(halves):
        loads[h].wait()
        total = jnp.zeros((part_i, LANES), jnp.float32)
        for k in range(steps):
            product = jnp.dot(
                tv[k, h * part_i : (h + 1) * part_i, :], weights, preferred_element_type=jnp.float32
            )
            total = total + product * c_rows[k : k + 1, :]
        total = total.T
        total = total[0:rank] + total[rank : 2 * rank]
        for q in range(groups):
            pbuf[q * halves + h] = total[q * SUBS : (q + 1) * SUBS]
        for step in range(1, n_ja):
            @pl.when(lax.rem(j + step, halves) == h)
            def _():
                ra_copies[step - 1].start()
    sends.extend(ra_copies)
    ra[j] = pbuf[j]

    arrived(gb_copies)
    gram_b = unpacked(functools.reduce(jnp.add, [gb[s] for s in range(n_ja)]), rank)
    solve_a = inverse(gram_b * gram_c)

    arrived(ra_copies)
    ga[j] = functools.reduce(jnp.add, [ra[s] for s in range(n_ja)])
    ga_copies = begin(spread(ga.at[j], ga, j, n_ja, on_ja, ga_s, ga_r))
    c_cols = [c_all[:, k : k + 1] for k in range(steps)]
    arrived(ga_copies)
    summed = stacked(
        [
            jnp.concatenate([ga[q * halves + h] for h in range(halves)], axis=1)
            for q in range(groups)
        ],
        rank,
    )
    raw_a = jnp.dot(solve_a[:, 0:rank], summed, precision=HIGH, preferred_element_type=jnp.float32)
    araw[...] = raw_a
    gr[a] = packed(wide_gram(raw_a))
    gr_copies = begin(spread(gr.at[a], gr, a, n_ia, on_ia, gr_s, gr_r))

    rb_copies = []
    pieces = []
    for k in range(steps):
        pieces.append(jnp.concatenate(split(raw_a * c_cols[k]), axis=0).astype(jnp.bfloat16))
    for h in range(cuts_j):
        total = jnp.zeros((2 * rank, part_j), jnp.float32)
        for k in range(steps):
            total = total + jnp.dot(
                pieces[k], tv[k, :, h * part_j : (h + 1) * part_j], preferred_element_type=jnp.float32
            )
        rb[h, a] = total[0:rank] + total[rank : 2 * rank]
        rb_copies.extend(
            begin(spread(rb.at[h, a], rb.at[h], a, n_ia, on_ia, rb_s.at[h], rb_r.at[h]))
        )

    arrived(gr_copies)
    gram_a = unpacked(functools.reduce(jnp.add, [gr[s] for s in range(n_ia)]), rank)
    lane = lax.broadcasted_iota(jnp.int32, (rank, LANES), 1)
    sub = lax.broadcasted_iota(jnp.int32, (rank, LANES), 0)
    squares = jnp.where(lane == sub, gram_a, 0.0)
    scale_col = 1.0 / jnp.sqrt(jnp.sum(squares, axis=1, keepdims=True) / total_i + EPS)
    scale_row = 1.0 / jnp.sqrt(jnp.sum(squares, axis=0, keepdims=True) / total_i + EPS)
    solve_b = inverse(gram_a * scale_col * scale_row * gram_c) * scale_row
    for q in range(n_ia):
        wsc[q] = solve_b[q * SUBS : (q + 1) * SUBS]
    new_a = araw[...] * scale_col
    for q in range(groups):
        araw[q * SUBS : (q + 1) * SUBS] = new_a[q * SUBS : (q + 1) * SUBS]
    height = rank // n_ja
    for p in range(n_ja):
        @pl.when(j == p)
        def _():
            oa_ref[...] = araw[p * height : (p + 1) * height, :]
    solve_own = wsc[a][:, 0:rank]

    arrived(rb_copies)
    raw_b = []
    for h in range(cuts_j):
        summed_b = functools.reduce(jnp.add, [rb[h, s] for s in range(n_ia)])
        raw_b.append(
            jnp.dot(solve_own, summed_b, precision=HIGH, preferred_element_type=jnp.float32)
        )
    raw_b = jnp.concatenate(raw_b, axis=1)
    sq[j] = jnp.broadcast_to(jnp.sum(raw_b * raw_b, axis=1, keepdims=True), (SUBS, LANES))
    sq_copies = begin(spread(sq.at[j], sq, j, n_ja, on_ja, sq_s, sq_r))
    arrived(sq_copies)
    squares_b = functools.reduce(jnp.add, [sq[s] for s in range(n_ja)])[:, 0:1]
    ob_ref[...] = raw_b / jnp.sqrt(squares_b / total_j + EPS)

    for copy in sends:
        copy.wait_send()


def fused(tensor, factor_b, factor_c):
    n_ia = lax.axis_size("ia")
    n_ja = lax.axis_size("ja")
    steps, width_i, width_j = tensor.shape
    rows_b = factor_b.shape[0]
    rank = rows_b * n_ia
    halves = n_ja // (rank // SUBS)
    cuts_j = 2
    f32 = jnp.float32
    vmem = pltpu.VMEM
    dma = pltpu.SemaphoreType.DMA
    ja_sems = [dma((n_ja,)), dma((n_ja,))]
    ia_sems = [dma((n_ia,)), dma((n_ia,))]
    scratch = [
        vmem(tensor.shape, tensor.dtype),
        vmem((n_ia, rows_b, width_j), f32),
        vmem(factor_c.shape, f32),
        vmem((SUBS, LANES), f32),
        vmem((n_ja, SUBS, LANES), f32),
        vmem((n_ia, n_ja, LANES), f32),
        vmem((n_ja, SUBS, LANES), f32),
        vmem((n_ja, SUBS, width_i // halves), f32),
        vmem((n_ja, SUBS, width_i // halves), f32),
        vmem((n_ja, SUBS, width_i // halves), f32),
        vmem((rank, width_i), f32),
        vmem((n_ia, SUBS, LANES), f32),
        vmem((cuts_j, n_ia, rank, width_j // cuts_j), f32),
        vmem((n_ia, SUBS, LANES), f32),
        vmem((n_ja, SUBS, LANES), f32),
        dma((halves,)),
        dma((2,)),
        *ia_sems, *ja_sems, *ia_sems, *ja_sems, *ja_sems, *ja_sems, *ia_sems,
        dma((cuts_j, n_ia)), dma((cuts_j, n_ia)),
        *ja_sems,
    ]
    flops = 8 * rank * tensor.size
    return pl.pallas_call(
        functools.partial(kernel, n_ia, n_ja, width_i * n_ia, width_j * n_ja),
        out_shape=(
            jax.ShapeDtypeStruct((rank // n_ja, width_i), f32),
            jax.ShapeDtypeStruct((rows_b, width_j), f32),
        ),
        in_specs=[
            pl.BlockSpec(memory_space=pltpu.HBM),
            pl.BlockSpec(memory_space=pltpu.HBM),
            pl.BlockSpec(memory_space=pltpu.HBM),
        ],
        out_specs=(pl.BlockSpec(memory_space=pltpu.VMEM), pl.BlockSpec(memory_space=pltpu.VMEM)),
        scratch_shapes=scratch,
        cost_estimate=pl.CostEstimate(flops=flops, bytes_accessed=2 * tensor.size, transcendentals=0),
        compiler_params=pltpu.CompilerParams(
            collective_id=0, has_side_effects=True, vmem_limit_bytes=24 * 2**20
        ),
    )(tensor, factor_b, factor_c)


def fits(mesh):
    n_ia, n_ja, n_ka = (mesh.shape[name] for name in ("ia", "ja", "ka"))
    return n_ka == 1 and n_ia * SUBS == 32 and n_ja % n_ia == 0 and n_ja <= SUBS


def solution(mesh):
    return jax.shard_map(
        fused if fits(mesh) else body,
        mesh=mesh,
        in_specs=(P("ka", "ia", "ja"), P("ia", ("ja", "ka")), P(("ia", "ja"), "ka")),
        out_specs=(P("ja", ("ia", "ka")), P("ia", ("ja", "ka"))),
        check_vma=False,
    )
```

```python
import functools

import jax
import jax.numpy as jnp
from jax import lax
from jax.experimental import pallas as pl
from jax.experimental.pallas import tpu as pltpu
from jax.sharding import PartitionSpec as P

EPS = 1e-06
HIGH = lax.Precision.HIGHEST


def gram_of(block):
    return jnp.dot(block, block.T, precision=HIGH, preferred_element_type=jnp.float32)


def solve_with(normal, rhs):
    lower = jnp.linalg.cholesky(normal)
    return jax.scipy.linalg.cho_solve((lower, True), rhs)


def arrange(partial_rows, rows_split, cols_split):
    rank, width = partial_rows.shape
    grid = partial_rows.reshape(rows_split, rank // rows_split, cols_split, width // cols_split)
    return grid.transpose(0, 2, 1, 3).reshape(rank * cols_split, width // cols_split)


def assemble(pieces, rows_split, cols_split):
    count, height, width = pieces.shape
    grid = pieces.reshape(rows_split, cols_split, height, width)
    return grid.transpose(0, 2, 1, 3).reshape(rows_split * height, cols_split * width)


def scaled(raw, squares, total):
    return raw / jnp.sqrt(squares / total + EPS)[:, None]


def body(tensor, factor_b, factor_c):
    n_ia = lax.axis_size("ia")
    n_ja = lax.axis_size("ja")
    n_ka = lax.axis_size("ka")
    total_i = tensor.shape[1] * n_ia
    total_j = tensor.shape[2] * n_ja
    c_block = lax.all_gather(factor_c, ("ia", "ja"), axis=0, tiled=True)
    pieces = lax.all_gather(factor_b[None], ("ia", "ka"), axis=0, tiled=True)
    b_block = assemble(pieces, n_ia, n_ka)
    gram_b = lax.psum(gram_of(b_block), "ja")
    gram_c = lax.psum(gram_of(c_block), "ka")
    normal_a = gram_b * gram_c
    kr_a = (c_block[:, :, None] * b_block[:, None, :]).astype(jnp.bfloat16)
    partial_a = jnp.einsum("rkj,kij->ri", kr_a, tensor, preferred_element_type=jnp.float32)
    solved_a = solve_with(normal_a, partial_a)
    raw_a = lax.psum_scatter(
        arrange(solved_a, n_ja, n_ka), ("ja", "ka"), scatter_dimension=0, tiled=True
    )
    squares_a = lax.psum(jnp.sum(raw_a * raw_a, axis=1), ("ia", "ka"))
    local_a = scaled(raw_a, squares_a, total_i)
    pieces_a = lax.all_gather(local_a[None], ("ja", "ka"), axis=0, tiled=True)
    gathered_a = assemble(pieces_a, n_ja, n_ka)
    gram_a = lax.psum(gram_of(gathered_a), "ia")
    normal_b = gram_a * gram_c
    kr_b = (c_block[:, :, None] * gathered_a[:, None, :]).astype(jnp.bfloat16)
    partial_b = jnp.einsum("rki,kij->rj", kr_b, tensor, preferred_element_type=jnp.float32)
    solved_b = solve_with(normal_b, partial_b)
    raw_b = lax.psum_scatter(
        arrange(solved_b, n_ia, n_ka), ("ia", "ka"), scatter_dimension=0, tiled=True
    )
    squares_b = lax.psum(jnp.sum(raw_b * raw_b, axis=1), ("ja", "ka"))
    share_b = scaled(raw_b, squares_b, total_j)
    return (local_a, share_b)


MESH = pl.DeviceIdType.MESH
LANES = 128
SUBS = 8
NT = (((1,), (1,)), ((), ()))


def spread(src, dst, me, count, device, send, recv):
    copies = []
    for step in range(1, count):
        copies.append(
            pltpu.make_async_remote_copy(
                src_ref=src,
                dst_ref=dst.at[me],
                send_sem=send.at[step],
                recv_sem=recv.at[step],
                device_id=device(lax.rem(me + step, count)),
                device_id_type=MESH,
            )
        )
    return copies


def stacked(pieces, rows):
    height, width = sum(p.shape[0] for p in pieces), pieces[0].shape[1]
    if rows > height:
        pieces = list(pieces) + [jnp.zeros((rows - height, width), pieces[0].dtype)]
    return jnp.concatenate(pieces, axis=0)


def wide_gram(block):
    other = stacked([block], LANES)
    return lax.dot_general(block, other, NT, precision=HIGH, preferred_element_type=jnp.float32)


def parts(values, rows):
    high = values.astype(jnp.bfloat16).astype(jnp.float32)
    rest = values - high
    middle = rest.astype(jnp.bfloat16).astype(jnp.float32)
    return stacked([high, middle, rest - middle], rows)


def folded(products, rank):
    total = products[0:rank] + products[rank : 2 * rank] + products[2 * rank : 3 * rank]
    return total + pltpu.roll(total, LANES - rank, 1) + pltpu.roll(total, LANES - 2 * rank, 1)


def masked(gram):
    lane = lax.broadcasted_iota(jnp.int32, gram.shape, 1)
    return jnp.where(lane < gram.shape[0], gram, 0.0)


def packed(gram):
    rank = gram.shape[0]
    tile = gram[0:SUBS]
    for q in range(1, rank // SUBS):
        tile = tile + pltpu.roll(gram[q * SUBS : (q + 1) * SUBS], q * rank, 1)
    return tile


def unpacked(tile, rank):
    lane = lax.broadcasted_iota(jnp.int32, (SUBS, LANES), 1)
    groups = []
    for q in range(rank // SUBS):
        moved = tile if q == 0 else pltpu.roll(tile, LANES - q * rank, 1)
        groups.append(jnp.where(lane < rank, moved, 0.0))
    return jnp.concatenate(groups, axis=0)


def inverse(normal):
    rank = normal.shape[0]
    blocks = [normal[q * SUBS : (q + 1) * SUBS] for q in range(rank // SUBS)]
    lane = lax.broadcasted_iota(jnp.int32, (SUBS, LANES), 1)
    sub = lax.broadcasted_iota(jnp.int32, (SUBS, LANES), 0)

    def column(block, index):
        return jnp.broadcast_to(block[:, index : index + 1], (SUBS, LANES))

    for q in range(rank // SUBS):
        first = q * SUBS
        cols = [[column(block, first + k) for k in range(SUBS)] for block in blocks]
        rows, inner = blocks[q], cols[q]
        for k in range(SUBS):
            col = inner[k]
            pivot = 1.0 / col[k : k + 1]
            row = jnp.where(lane[0:1] == first + k, 1.0, rows[k : k + 1]) * pivot
            rest = jnp.where(lane == first + k, 0.0, rows) - col * row
            rows = jnp.where(sub == k, row, rest)
            for m in range(k + 1, SUBS):
                entry = inner[m][k : k + 1] * pivot
                inner[m] = jnp.where(sub == k, entry, inner[m] - col * entry)
        inside = (lane >= first) & (lane < first + SUBS)
        for p in range(rank // SUBS):
            if p != q:
                total = jnp.where(inside, 0.0, blocks[p])
                for k in range(SUBS):
                    total = total - cols[p][k] * rows[k : k + 1]
                blocks[p] = total
        blocks[q] = rows
    return jnp.concatenate(blocks, axis=0)


def split(values):
    high = values.astype(jnp.bfloat16).astype(jnp.float32)
    return high, values - high


def kernel(
    n_ia, n_ja, total_i, total_j,
    t_ref, b_ref, c_ref, oa_ref, ob_ref,
    tv, ball, cin, cst, cja, cia, gb, pbuf, ra, ga, araw, gr, rb, wsc, sq, prod,
    t_sem, in_sem, b_s, b_r, cj_s, cj_r, ci_s, ci_r, gb_s, gb_r, ra_s, ra_r, ga_s, ga_r,
    gr_s, gr_r, rb_s, rb_r, sq_s, sq_r,
):
    a = lax.axis_index("ia")
    j = lax.axis_index("ja")
    steps, width_i, width_j = tv.shape
    rank = n_ia * b_ref.shape[0]
    groups = rank // SUBS
    halves = n_ja // groups
    part_i = width_i // halves
    cuts_j = rb.shape[0]
    part_j = width_j // cuts_j

    def on_ia(index):
        return (index, j, 0)

    def on_ja(index):
        return (a, index, 0)

    fetch_c = pltpu.make_async_copy(c_ref, cin, in_sem.at[0])
    fetch_b = pltpu.make_async_copy(b_ref, ball.at[a], in_sem.at[1])
    fetch_c.start()
    fetch_b.start()
    loads = []
    for h in range(halves):
        rows = pl.ds(h * part_i, part_i)
        load = pltpu.make_async_copy(t_ref.at[:, rows], tv.at[:, rows], t_sem.at[h])
        load.start()
        loads.append(load)

    barrier = pltpu.get_barrier_semaphore()
    for step in range(1, n_ia):
        pl.semaphore_signal(barrier, inc=1, device_id=on_ia(lax.rem(a + step, n_ia)), device_id_type=MESH)
    for step in range(1, n_ja):
        pl.semaphore_signal(barrier, inc=1, device_id=on_ja(lax.rem(j + step, n_ja)), device_id_type=MESH)
    cst[...] = jnp.zeros_like(cst)
    fetch_c.wait()
    cst[0:1, 0:steps] = cin[...]
    cja[j] = cst[...]
    fetch_b.wait()
    pl.semaphore_wait(barrier, n_ia + n_ja - 2)

    sends = []

    def begin(copies):
        for copy in copies:
            copy.start()
        sends.extend(copies)
        return copies

    def arrived(copies):
        for copy in copies:
            copy.wait_recv()

    cj_copies = begin(spread(cst, cja, j, n_ja, on_ja, cj_s, cj_r))
    b_copies = begin(spread(ball.at[a], ball, a, n_ia, on_ia, b_s, b_r))
    arrived(cj_copies)
    cia[a] = stacked([cja[s, 0:1, :] for s in range(n_ja)], n_ja)
    ci_copies = begin(spread(cia.at[a], cia, a, n_ia, on_ia, ci_s, ci_r))
    arrived(b_copies)
    b_parts = parts(stacked([ball[s] for s in range(n_ia)], rank), LANES)
    weights = b_parts.T.astype(jnp.bfloat16)

    ra_copies = []
    for step in range(1, n_ja):
        peer = lax.rem(j + step, n_ja)
        ra_copies.append(
            pltpu.make_async_remote_copy(
                src_ref=pbuf.at[peer],
                dst_ref=ra.at[j],
                send_sem=ra_s.at[step],
                recv_sem=ra_r.at[step],
                device_id=on_ja(peer),
                device_id_type=MESH,
            )
        )

    def product_a(h, k):
        return jnp.dot(
            tv[k, h * part_i : (h + 1) * part_i, :], weights, preferred_element_type=jnp.float32
        )

    loads[0].wait()
    for k in range(steps):
        prod[k] = product_a(0, k)
    gb[j] = packed(
        masked(
            folded(
                jnp.dot(b_parts.astype(jnp.bfloat16), weights, preferred_element_type=jnp.float32),
                rank,
            )
        )
    )
    gb_copies = begin(spread(gb.at[j], gb, j, n_ja, on_ja, gb_s, gb_r))
    arrived(ci_copies)
    c_all = stacked([cia[s] for s in range(n_ia)], rank)
    c_rows = stacked([c_all, c_all, c_all], LANES).T
    for h in range(halves):
        if h:
            loads[h].wait()
        total = jnp.zeros((part_i, LANES), jnp.float32)
        for k in range(steps):
            product = product_a(h, k) if h else prod[k]
            total = total + product * c_rows[k : k + 1, :]
        total = total.T
        total = total[0:rank] + total[rank : 2 * rank] + total[2 * rank : 3 * rank]
        for q in range(groups):
            pbuf[q * halves + h] = total[q * SUBS : (q + 1) * SUBS]
        for step in range(1, n_ja):
            @pl.when(lax.rem(j + step, halves) == h)
            def _():
                ra_copies[step - 1].start()
    sends.extend(ra_copies)
    ra[j] = pbuf[j]
    gram_c = wide_gram(c_all)

    arrived(gb_copies)
    gram_b = unpacked(functools.reduce(jnp.add, [gb[s] for s in range(n_ja)]), rank)
    solve_a = inverse(gram_b * gram_c)

    arrived(ra_copies)
    ga[j] = functools.reduce(jnp.add, [ra[s] for s in range(n_ja)])
    ga_copies = begin(spread(ga.at[j], ga, j, n_ja, on_ja, ga_s, ga_r))
    c_cols = [c_all[:, k : k + 1] for k in range(steps)]
    arrived(ga_copies)
    summed = stacked(
        [
            jnp.concatenate([ga[q * halves + h] for h in range(halves)], axis=1)
            for q in range(groups)
        ],
        rank,
    )
    raw_a = jnp.dot(solve_a[:, 0:rank], summed, precision=HIGH, preferred_element_type=jnp.float32)
    araw[...] = raw_a
    a_parts = parts(raw_a, LANES).astype(jnp.bfloat16)
    products = lax.dot_general(a_parts, a_parts, NT, preferred_element_type=jnp.float32)
    gr[a] = packed(masked(folded(products, rank)))
    gr_copies = begin(spread(gr.at[a], gr, a, n_ia, on_ia, gr_s, gr_r))

    rb_copies = []
    pieces = []
    for k in range(steps):
        pieces.append(jnp.concatenate(split(raw_a * c_cols[k]), axis=0).astype(jnp.bfloat16))
    for h in range(cuts_j):
        total = jnp.zeros((2 * rank, part_j), jnp.float32)
        for k in range(steps):
            total = total + jnp.dot(
                pieces[k], tv[k, :, h * part_j : (h + 1) * part_j], preferred_element_type=jnp.float32
            )
        rb[h, a] = total[0:rank] + total[rank : 2 * rank]
        rb_copies.extend(
            begin(spread(rb.at[h, a], rb.at[h], a, n_ia, on_ia, rb_s.at[h], rb_r.at[h]))
        )

    arrived(gr_copies)
    gram_a = unpacked(functools.reduce(jnp.add, [gr[s] for s in range(n_ia)]), rank)
    lane = lax.broadcasted_iota(jnp.int32, (rank, LANES), 1)
    sub = lax.broadcasted_iota(jnp.int32, (rank, LANES), 0)
    squares = jnp.where(lane == sub, gram_a, 0.0)
    scale_col = 1.0 / jnp.sqrt(jnp.sum(squares, axis=1, keepdims=True) / total_i + EPS)
    scale_row = 1.0 / jnp.sqrt(jnp.sum(squares, axis=0, keepdims=True) / total_i + EPS)
    solve_b = inverse(gram_a * scale_col * scale_row * gram_c) * scale_row
    for q in range(n_ia):
        wsc[q] = solve_b[q * SUBS : (q + 1) * SUBS]
    new_a = araw[...] * scale_col
    for q in range(groups):
        araw[q * SUBS : (q + 1) * SUBS] = new_a[q * SUBS : (q + 1) * SUBS]
    height = rank // n_ja
    for p in range(n_ja):
        @pl.when(j == p)
        def _():
            oa_ref[...] = araw[p * height : (p + 1) * height, :]
    solve_own = wsc[a][:, 0:rank]

    arrived(rb_copies)
    raw_b = []
    for h in range(cuts_j):
        summed_b = functools.reduce(jnp.add, [rb[h, s] for s in range(n_ia)])
        raw_b.append(
            jnp.dot(solve_own, summed_b, precision=HIGH, preferred_element_type=jnp.float32)
        )
    raw_b = jnp.concatenate(raw_b, axis=1)
    sq[j] = jnp.broadcast_to(jnp.sum(raw_b * raw_b, axis=1, keepdims=True), (SUBS, LANES))
    sq_copies = begin(spread(sq.at[j], sq, j, n_ja, on_ja, sq_s, sq_r))
    arrived(sq_copies)
    squares_b = functools.reduce(jnp.add, [sq[s] for s in range(n_ja)])[:, 0:1]
    ob_ref[...] = raw_b / jnp.sqrt(squares_b / total_j + EPS)

    for copy in sends:
        copy.wait_send()


def fused(tensor, factor_b, factor_c):
    n_ia = lax.axis_size("ia")
    n_ja = lax.axis_size("ja")
    steps, width_i, width_j = tensor.shape
    rows_b = factor_b.shape[0]
    rank = rows_b * n_ia
    halves = n_ja // (rank // SUBS)
    cuts_j = 2
    f32 = jnp.float32
    vmem = pltpu.VMEM
    dma = pltpu.SemaphoreType.DMA
    ja_sems = [dma((n_ja,)), dma((n_ja,))]
    ia_sems = [dma((n_ia,)), dma((n_ia,))]
    scratch = [
        vmem(tensor.shape, tensor.dtype),
        vmem((n_ia, rows_b, width_j), f32),
        vmem(factor_c.shape, f32),
        vmem((SUBS, LANES), f32),
        vmem((n_ja, SUBS, LANES), f32),
        vmem((n_ia, n_ja, LANES), f32),
        vmem((n_ja, SUBS, LANES), f32),
        vmem((n_ja, SUBS, width_i // halves), f32),
        vmem((n_ja, SUBS, width_i // halves), f32),
        vmem((n_ja, SUBS, width_i // halves), f32),
        vmem((rank, width_i), f32),
        vmem((n_ia, SUBS, LANES), f32),
        vmem((cuts_j, n_ia, rank, width_j // cuts_j), f32),
        vmem((n_ia, SUBS, LANES), f32),
        vmem((n_ja, SUBS, LANES), f32),
        vmem((steps, width_i // halves, LANES), f32),
        dma((halves,)),
        dma((2,)),
        *ia_sems, *ja_sems, *ia_sems, *ja_sems, *ja_sems, *ja_sems, *ia_sems,
        dma((cuts_j, n_ia)), dma((cuts_j, n_ia)),
        *ja_sems,
    ]
    flops = 8 * rank * tensor.size
    return pl.pallas_call(
        functools.partial(kernel, n_ia, n_ja, width_i * n_ia, width_j * n_ja),
        out_shape=(
            jax.ShapeDtypeStruct((rank // n_ja, width_i), f32),
            jax.ShapeDtypeStruct((rows_b, width_j), f32),
        ),
        in_specs=[
            pl.BlockSpec(memory_space=pltpu.HBM),
            pl.BlockSpec(memory_space=pltpu.HBM),
            pl.BlockSpec(memory_space=pltpu.HBM),
        ],
        out_specs=(pl.BlockSpec(memory_space=pltpu.VMEM), pl.BlockSpec(memory_space=pltpu.VMEM)),
        scratch_shapes=scratch,
        cost_estimate=pl.CostEstimate(flops=flops, bytes_accessed=2 * tensor.size, transcendentals=0),
        compiler_params=pltpu.CompilerParams(
            collective_id=0, has_side_effects=True, vmem_limit_bytes=56 * 2**20
        ),
    )(tensor, factor_b, factor_c)


def fits(mesh):
    n_ia, n_ja, n_ka = (mesh.shape[name] for name in ("ia", "ja", "ka"))
    return n_ka == 1 and n_ia * SUBS == 32 and n_ja % n_ia == 0 and n_ja <= SUBS


def solution(mesh):
    return jax.shard_map(
        fused if fits(mesh) else body,
        mesh=mesh,
        in_specs=(P("ka", "ia", "ja"), P("ia", ("ja", "ka")), P(("ia", "ja"), "ka")),
        out_specs=(P("ja", ("ia", "ka")), P("ia", ("ja", "ka"))),
        check_vma=False,
    )
```

```python
import functools

import jax
import jax.numpy as jnp
from jax import lax
from jax.experimental import pallas as pl
from jax.experimental.pallas import tpu as pltpu
from jax.sharding import PartitionSpec as P

EPS = 1e-06
HIGH = lax.Precision.HIGHEST


def gram_of(block):
    return jnp.dot(block, block.T, precision=HIGH, preferred_element_type=jnp.float32)


def solve_with(normal, rhs):
    lower = jnp.linalg.cholesky(normal)
    return jax.scipy.linalg.cho_solve((lower, True), rhs)


def arrange(partial_rows, rows_split, cols_split):
    rank, width = partial_rows.shape
    grid = partial_rows.reshape(rows_split, rank // rows_split, cols_split, width // cols_split)
    return grid.transpose(0, 2, 1, 3).reshape(rank * cols_split, width // cols_split)


def assemble(pieces, rows_split, cols_split):
    count, height, width = pieces.shape
    grid = pieces.reshape(rows_split, cols_split, height, width)
    return grid.transpose(0, 2, 1, 3).reshape(rows_split * height, cols_split * width)


def scaled(raw, squares, total):
    return raw / jnp.sqrt(squares / total + EPS)[:, None]


def body(tensor, factor_b, factor_c):
    n_ia = lax.axis_size("ia")
    n_ja = lax.axis_size("ja")
    n_ka = lax.axis_size("ka")
    total_i = tensor.shape[1] * n_ia
    total_j = tensor.shape[2] * n_ja
    c_block = lax.all_gather(factor_c, ("ia", "ja"), axis=0, tiled=True)
    pieces = lax.all_gather(factor_b[None], ("ia", "ka"), axis=0, tiled=True)
    b_block = assemble(pieces, n_ia, n_ka)
    gram_b = lax.psum(gram_of(b_block), "ja")
    gram_c = lax.psum(gram_of(c_block), "ka")
    normal_a = gram_b * gram_c
    kr_a = (c_block[:, :, None] * b_block[:, None, :]).astype(jnp.bfloat16)
    partial_a = jnp.einsum("rkj,kij->ri", kr_a, tensor, preferred_element_type=jnp.float32)
    solved_a = solve_with(normal_a, partial_a)
    raw_a = lax.psum_scatter(
        arrange(solved_a, n_ja, n_ka), ("ja", "ka"), scatter_dimension=0, tiled=True
    )
    squares_a = lax.psum(jnp.sum(raw_a * raw_a, axis=1), ("ia", "ka"))
    local_a = scaled(raw_a, squares_a, total_i)
    pieces_a = lax.all_gather(local_a[None], ("ja", "ka"), axis=0, tiled=True)
    gathered_a = assemble(pieces_a, n_ja, n_ka)
    gram_a = lax.psum(gram_of(gathered_a), "ia")
    normal_b = gram_a * gram_c
    kr_b = (c_block[:, :, None] * gathered_a[:, None, :]).astype(jnp.bfloat16)
    partial_b = jnp.einsum("rki,kij->rj", kr_b, tensor, preferred_element_type=jnp.float32)
    solved_b = solve_with(normal_b, partial_b)
    raw_b = lax.psum_scatter(
        arrange(solved_b, n_ia, n_ka), ("ia", "ka"), scatter_dimension=0, tiled=True
    )
    squares_b = lax.psum(jnp.sum(raw_b * raw_b, axis=1), ("ja", "ka"))
    share_b = scaled(raw_b, squares_b, total_j)
    return (local_a, share_b)


MESH = pl.DeviceIdType.MESH
LANES = 128
SUBS = 8
NT = (((1,), (1,)), ((), ()))


def spread(src, dst, me, count, device, send, recv):
    copies = []
    for step in range(1, count):
        copies.append(
            pltpu.make_async_remote_copy(
                src_ref=src,
                dst_ref=dst.at[me],
                send_sem=send.at[step],
                recv_sem=recv.at[step],
                device_id=device(lax.rem(me + step, count)),
                device_id_type=MESH,
            )
        )
    return copies


def stacked(pieces, rows):
    height, width = sum(p.shape[0] for p in pieces), pieces[0].shape[1]
    if rows > height:
        pieces = list(pieces) + [jnp.zeros((rows - height, width), pieces[0].dtype)]
    return jnp.concatenate(pieces, axis=0)


def wide_gram(block):
    other = stacked([block], LANES)
    return lax.dot_general(block, other, NT, precision=HIGH, preferred_element_type=jnp.float32)


def parts(values, rows):
    high = values.astype(jnp.bfloat16).astype(jnp.float32)
    rest = values - high
    middle = rest.astype(jnp.bfloat16).astype(jnp.float32)
    return stacked([high, middle, rest - middle], rows)


def folded(products, rank):
    total = products[0:rank] + products[rank : 2 * rank] + products[2 * rank : 3 * rank]
    return total + pltpu.roll(total, LANES - rank, 1) + pltpu.roll(total, LANES - 2 * rank, 1)


def masked(gram):
    lane = lax.broadcasted_iota(jnp.int32, gram.shape, 1)
    return jnp.where(lane < gram.shape[0], gram, 0.0)


def packed(gram):
    rank = gram.shape[0]
    tile = gram[0:SUBS]
    for q in range(1, rank // SUBS):
        tile = tile + pltpu.roll(gram[q * SUBS : (q + 1) * SUBS], q * rank, 1)
    return tile


def unpacked(tile, rank):
    lane = lax.broadcasted_iota(jnp.int32, (SUBS, LANES), 1)
    groups = []
    for q in range(rank // SUBS):
        moved = tile if q == 0 else pltpu.roll(tile, LANES - q * rank, 1)
        groups.append(jnp.where(lane < rank, moved, 0.0))
    return jnp.concatenate(groups, axis=0)


def inverse(normal):
    rank = normal.shape[0]
    blocks = [normal[q * SUBS : (q + 1) * SUBS] for q in range(rank // SUBS)]
    lane = lax.broadcasted_iota(jnp.int32, (SUBS, LANES), 1)
    sub = lax.broadcasted_iota(jnp.int32, (SUBS, LANES), 0)

    def column(block, index):
        return jnp.broadcast_to(block[:, index : index + 1], (SUBS, LANES))

    for q in range(rank // SUBS):
        first = q * SUBS
        cols = [[column(block, first + k) for k in range(SUBS)] for block in blocks]
        rows, inner = blocks[q], cols[q]
        for k in range(SUBS):
            col = inner[k]
            pivot = 1.0 / col[k : k + 1]
            row = jnp.where(lane[0:1] == first + k, 1.0, rows[k : k + 1]) * pivot
            rest = jnp.where(lane == first + k, 0.0, rows) - col * row
            rows = jnp.where(sub == k, row, rest)
            for m in range(k + 1, SUBS):
                entry = inner[m][k : k + 1] * pivot
                inner[m] = jnp.where(sub == k, entry, inner[m] - col * entry)
        inside = (lane >= first) & (lane < first + SUBS)
        for p in range(rank // SUBS):
            if p != q:
                total = jnp.where(inside, 0.0, blocks[p])
                for k in range(SUBS):
                    total = total - cols[p][k] * rows[k : k + 1]
                blocks[p] = total
        blocks[q] = rows
    return jnp.concatenate(blocks, axis=0)


def split(values):
    high = values.astype(jnp.bfloat16).astype(jnp.float32)
    return high, values - high


def kernel(
    n_ia, n_ja, total_i, total_j,
    t_ref, b_ref, c_ref, oa_ref, ob_ref,
    tv, ball, cin, cs, gb, pbuf, ra, ga, araw, gr, pb, rb, wsc, sq, rs, rf, prod,
    t_sem, in_sem, b_s, b_r, c_s, c_r, gb_s, gb_r, ra_s, ra_r, ga_s, ga_r,
    gr_s, gr_r, rb_s, rb_r, sq_s, sq_r, rf_s, rf_r,
):
    a = lax.axis_index("ia")
    j = lax.axis_index("ja")
    steps, width_i, width_j = tv.shape
    rank = n_ia * b_ref.shape[0]
    groups = rank // SUBS
    halves = n_ja // groups
    part_i = width_i // halves
    cuts_j = 2
    part_j = width_j // cuts_j
    piece_j = width_j // n_ia

    n_all = n_ia * n_ja
    mine = a * n_ja + j

    def on_all(index):
        return (index // n_ja, lax.rem(index, n_ja), 0)

    def on_ia(index):
        return (index, j, 0)

    def on_ja(index):
        return (a, index, 0)

    fetch_c = pltpu.make_async_copy(c_ref, cin, in_sem.at[0])
    fetch_b = pltpu.make_async_copy(b_ref, ball.at[a], in_sem.at[1])
    fetch_c.start()
    fetch_b.start()
    loads = []
    for h in range(halves):
        rows = pl.ds(h * part_i, part_i)
        load = pltpu.make_async_copy(t_ref.at[:, rows], tv.at[:, rows], t_sem.at[h])
        load.start()
        loads.append(load)

    barrier = pltpu.get_barrier_semaphore()
    for step in range(1, n_all):
        pl.semaphore_signal(barrier, inc=1, device_id=on_all(lax.rem(mine + step, n_all)), device_id_type=MESH)
    fetch_c.wait()
    cs[mine] = jnp.zeros((1, LANES), jnp.float32)
    cs[mine, :, 0:steps] = cin[...]
    fetch_b.wait()
    pl.semaphore_wait(barrier, n_all - 1)

    sends = []

    def begin(copies):
        for copy in copies:
            copy.start()
        sends.extend(copies)
        return copies

    def arrived(copies):
        for copy in copies:
            copy.wait_recv()

    b_copies = begin(spread(ball.at[a], ball, a, n_ia, on_ia, b_s, b_r))
    c_copies = begin(spread(cs.at[mine], cs, mine, n_all, on_all, c_s, c_r))
    arrived(b_copies)
    b_parts = parts(stacked([ball[s] for s in range(n_ia)], rank), LANES)
    weights = b_parts.T.astype(jnp.bfloat16)

    ra_copies = []
    for step in range(1, n_ja):
        peer = lax.rem(j + step, n_ja)
        ra_copies.append(
            pltpu.make_async_remote_copy(
                src_ref=pbuf.at[peer],
                dst_ref=ra.at[j],
                send_sem=ra_s.at[step],
                recv_sem=ra_r.at[step],
                device_id=on_ja(peer),
                device_id_type=MESH,
            )
        )

    def product_a(h, k):
        return jnp.dot(
            tv[k, h * part_i : (h + 1) * part_i, :], weights, preferred_element_type=jnp.float32
        )

    loads[0].wait()
    for k in range(steps):
        prod[k] = product_a(0, k)
    gb[j] = packed(
        masked(
            folded(
                jnp.dot(b_parts.astype(jnp.bfloat16), weights, preferred_element_type=jnp.float32),
                rank,
            )
        )
    )
    gb_copies = begin(spread(gb.at[j], gb, j, n_ja, on_ja, gb_s, gb_r))
    arrived(c_copies)
    c_all = stacked([cs[s] for s in range(n_all)], rank)
    c_rows = stacked([c_all, c_all, c_all], LANES).T
    for h in range(halves):
        if h:
            loads[h].wait()
        total = jnp.zeros((part_i, LANES), jnp.float32)
        for k in range(steps):
            product = product_a(h, k) if h else prod[k]
            total = total + product * c_rows[k : k + 1, :]
        total = total.T
        total = total[0:rank] + total[rank : 2 * rank] + total[2 * rank : 3 * rank]
        for q in range(groups):
            pbuf[q * halves + h] = total[q * SUBS : (q + 1) * SUBS]
        for step in range(1, n_ja):
            @pl.when(lax.rem(j + step, halves) == h)
            def _():
                ra_copies[step - 1].start()
    sends.extend(ra_copies)
    ra[j] = pbuf[j]
    gram_c = wide_gram(c_all)

    arrived(gb_copies)
    gram_b = unpacked(functools.reduce(jnp.add, [gb[s] for s in range(n_ja)]), rank)
    solve_a = inverse(gram_b * gram_c)

    arrived(ra_copies)
    ga[j] = functools.reduce(jnp.add, [ra[s] for s in range(n_ja)])
    ga_copies = begin(spread(ga.at[j], ga, j, n_ja, on_ja, ga_s, ga_r))
    c_cols = [c_all[:, k : k + 1] for k in range(steps)]
    arrived(ga_copies)
    summed = stacked(
        [
            jnp.concatenate([ga[q * halves + h] for h in range(halves)], axis=1)
            for q in range(groups)
        ],
        rank,
    )
    raw_a = jnp.dot(solve_a[:, 0:rank], summed, precision=HIGH, preferred_element_type=jnp.float32)
    araw[...] = raw_a
    a_parts = parts(raw_a, LANES).astype(jnp.bfloat16)
    products = lax.dot_general(a_parts, a_parts, NT, preferred_element_type=jnp.float32)
    gr[a] = packed(masked(folded(products, rank)))
    gr_copies = begin(spread(gr.at[a], gr, a, n_ia, on_ia, gr_s, gr_r))

    rb_copies = []
    for step in range(1, n_ia):
        peer = lax.rem(a + step, n_ia)
        rb_copies.append(
            pltpu.make_async_remote_copy(
                src_ref=pb.at[peer],
                dst_ref=rb.at[a],
                send_sem=rb_s.at[step],
                recv_sem=rb_r.at[step],
                device_id=on_ia(peer),
                device_id_type=MESH,
            )
        )
    pieces = []
    for k in range(steps):
        pieces.append(jnp.concatenate(split(raw_a * c_cols[k]), axis=0).astype(jnp.bfloat16))
    for h in range(cuts_j):
        total = jnp.zeros((2 * rank, part_j), jnp.float32)
        for k in range(steps):
            total = total + jnp.dot(
                pieces[k], tv[k, :, h * part_j : (h + 1) * part_j], preferred_element_type=jnp.float32
            )
        total = total[0:rank] + total[rank : 2 * rank]
        for m in range(n_ia // cuts_j):
            pb[h * (n_ia // cuts_j) + m] = total[:, m * piece_j : (m + 1) * piece_j]
        for step in range(1, n_ia):
            @pl.when(lax.rem(a + step, n_ia) // (n_ia // cuts_j) == h)
            def _():
                rb_copies[step - 1].start()
    sends.extend(rb_copies)
    rb[a] = pb[a]

    arrived(gr_copies)
    gram_a = unpacked(functools.reduce(jnp.add, [gr[s] for s in range(n_ia)]), rank)
    lane = lax.broadcasted_iota(jnp.int32, (rank, LANES), 1)
    sub = lax.broadcasted_iota(jnp.int32, (rank, LANES), 0)
    squares = jnp.where(lane == sub, gram_a, 0.0)
    scale_col = 1.0 / jnp.sqrt(jnp.sum(squares, axis=1, keepdims=True) / total_i + EPS)
    scale_row = 1.0 / jnp.sqrt(jnp.sum(squares, axis=0, keepdims=True) / total_i + EPS)
    solve_b = inverse(gram_a * scale_col * scale_row * gram_c) * scale_row
    new_a = araw[...] * scale_col
    for q in range(groups):
        araw[q * SUBS : (q + 1) * SUBS] = new_a[q * SUBS : (q + 1) * SUBS]
    height = rank // n_ja
    for p in range(n_ja):
        @pl.when(j == p)
        def _():
            oa_ref[...] = araw[p * height : (p + 1) * height, :]

    arrived(rb_copies)
    summed_b = functools.reduce(jnp.add, [rb[s] for s in range(n_ia)])
    raw_b = jnp.dot(solve_b[:, 0:rank], summed_b, precision=HIGH, preferred_element_type=jnp.float32)
    sums = jnp.sum(raw_b * raw_b, axis=1, keepdims=True)
    sq[mine] = jnp.sum(jnp.where(lane == sub, sums, 0.0), axis=0, keepdims=True)
    for q in range(n_ia):
        rs[q] = raw_b[q * SUBS : (q + 1) * SUBS]
    rf[a] = rs[a]
    sq_copies = spread(sq.at[mine], sq, mine, n_all, on_all, sq_s, sq_r)
    rf_copies = []
    for step in range(1, n_ia):
        peer = lax.rem(a + step, n_ia)
        rf_copies.append(
            pltpu.make_async_remote_copy(
                src_ref=rs.at[peer],
                dst_ref=rf.at[a],
                send_sem=rf_s.at[step],
                recv_sem=rf_r.at[step],
                device_id=on_ia(peer),
                device_id_type=MESH,
            )
        )
    begin(rf_copies)
    begin(sq_copies)
    arrived(rf_copies)
    arrived(sq_copies)
    squares_b = functools.reduce(jnp.add, [sq[s] for s in range(n_all)])
    total_b = jnp.sum(jnp.where(lane == sub, squares_b, 0.0), axis=1, keepdims=True)
    scale_b = jnp.broadcast_to(1.0 / jnp.sqrt(total_b / total_j + EPS), (rank, LANES))
    for q in range(n_ia):
        wsc[q] = scale_b[q * SUBS : (q + 1) * SUBS]
    own = wsc[a]
    for q in range(n_ia):
        ob_ref[:, q * piece_j : (q + 1) * piece_j] = rf[q] * own

    for copy in sends:
        copy.wait_send()


def write_out(a_ref, b_ref, oa_ref, ob_ref, sems):
    copies = [
        pltpu.make_async_copy(a_ref, oa_ref, sems.at[0]),
        pltpu.make_async_copy(b_ref, ob_ref, sems.at[1]),
    ]
    for copy in copies:
        copy.start()
    for copy in copies:
        copy.wait()


def fused(tensor, factor_b, factor_c):
    n_ia = lax.axis_size("ia")
    n_ja = lax.axis_size("ja")
    steps, width_i, width_j = tensor.shape
    rows_b = factor_b.shape[0]
    rank = rows_b * n_ia
    halves = n_ja // (rank // SUBS)
    f32 = jnp.float32
    vmem = pltpu.VMEM
    dma = pltpu.SemaphoreType.DMA
    ja_sems = [dma((n_ja,)), dma((n_ja,))]
    ia_sems = [dma((n_ia,)), dma((n_ia,))]
    all_sems = [dma((n_ia * n_ja,)), dma((n_ia * n_ja,))]
    scratch = [
        vmem(tensor.shape, tensor.dtype),
        vmem((n_ia, rows_b, width_j), f32),
        vmem(factor_c.shape, f32),
        vmem((n_ia * n_ja, 1, LANES), f32),
        vmem((n_ja, SUBS, LANES), f32),
        vmem((n_ja, SUBS, width_i // halves), f32),
        vmem((n_ja, SUBS, width_i // halves), f32),
        vmem((n_ja, SUBS, width_i // halves), f32),
        vmem((rank, width_i), f32),
        vmem((n_ia, SUBS, LANES), f32),
        vmem((n_ia, rank, width_j // n_ia), f32),
        vmem((n_ia, rank, width_j // n_ia), f32),
        vmem((n_ia, SUBS, LANES), f32),
        vmem((n_ia * n_ja, 1, LANES), f32),
        vmem((n_ia, SUBS, width_j // n_ia), f32),
        vmem((n_ia, SUBS, width_j // n_ia), f32),
        vmem((steps, width_i // halves, LANES), f32),
        dma((halves,)),
        dma((2,)),
        *ia_sems, *all_sems, *ja_sems, *ja_sems, *ja_sems, *ia_sems, *ia_sems, *all_sems, *ia_sems,
    ]
    flops = 8 * rank * tensor.size
    results = pl.pallas_call(
        functools.partial(kernel, n_ia, n_ja, width_i * n_ia, width_j * n_ja),
        out_shape=(
            jax.ShapeDtypeStruct((rank // n_ja, width_i), f32),
            jax.ShapeDtypeStruct((rows_b, width_j), f32),
        ),
        in_specs=[
            pl.BlockSpec(memory_space=pltpu.HBM),
            pl.BlockSpec(memory_space=pltpu.HBM),
            pl.BlockSpec(memory_space=pltpu.HBM),
        ],
        out_specs=(pl.BlockSpec(memory_space=pltpu.VMEM), pl.BlockSpec(memory_space=pltpu.VMEM)),
        scratch_shapes=scratch,
        cost_estimate=pl.CostEstimate(flops=flops, bytes_accessed=2 * tensor.size, transcendentals=0),
        compiler_params=pltpu.CompilerParams(
            collective_id=0, has_side_effects=True, vmem_limit_bytes=56 * 2**20
        ),
    )(tensor, factor_b, factor_c)
    anywhere = pl.BlockSpec(memory_space=pl.ANY)
    return pl.pallas_call(
        write_out,
        out_shape=tuple(jax.ShapeDtypeStruct(r.shape, r.dtype) for r in results),
        in_specs=[anywhere, anywhere],
        out_specs=(anywhere, anywhere),
        scratch_shapes=[dma((2,))],
        compiler_params=pltpu.CompilerParams(vmem_limit_bytes=56 * 2**20),
    )(*results)


def fits(mesh):
    n_ia, n_ja, n_ka = (mesh.shape[name] for name in ("ia", "ja", "ka"))
    return n_ka == 1 and n_ia * SUBS == 32 and n_ja == 2 * n_ia


def solution(mesh):
    return jax.shard_map(
        fused if fits(mesh) else body,
        mesh=mesh,
        in_specs=(P("ka", "ia", "ja"), P("ia", ("ja", "ka")), P(("ia", "ja"), "ka")),
        out_specs=(P("ja", ("ia", "ka")), P("ia", ("ja", "ka"))),
        check_vma=False,
    )
```

```python
import functools

import jax
import jax.numpy as jnp
from jax import lax
from jax.experimental import pallas as pl
from jax.experimental.pallas import tpu as pltpu
from jax.sharding import PartitionSpec as P

EPS = 1e-06
HIGH = lax.Precision.HIGHEST


def gram_of(block):
    return jnp.dot(block, block.T, precision=HIGH, preferred_element_type=jnp.float32)


def solve_with(normal, rhs):
    lower = jnp.linalg.cholesky(normal)
    return jax.scipy.linalg.cho_solve((lower, True), rhs)


def arrange(partial_rows, rows_split, cols_split):
    rank, width = partial_rows.shape
    grid = partial_rows.reshape(rows_split, rank // rows_split, cols_split, width // cols_split)
    return grid.transpose(0, 2, 1, 3).reshape(rank * cols_split, width // cols_split)


def assemble(pieces, rows_split, cols_split):
    count, height, width = pieces.shape
    grid = pieces.reshape(rows_split, cols_split, height, width)
    return grid.transpose(0, 2, 1, 3).reshape(rows_split * height, cols_split * width)


def scaled(raw, squares, total):
    return raw / jnp.sqrt(squares / total + EPS)[:, None]


def body(tensor, factor_b, factor_c):
    n_ia = lax.axis_size("ia")
    n_ja = lax.axis_size("ja")
    n_ka = lax.axis_size("ka")
    total_i = tensor.shape[1] * n_ia
    total_j = tensor.shape[2] * n_ja
    c_block = lax.all_gather(factor_c, ("ia", "ja"), axis=0, tiled=True)
    pieces = lax.all_gather(factor_b[None], ("ia", "ka"), axis=0, tiled=True)
    b_block = assemble(pieces, n_ia, n_ka)
    gram_b = lax.psum(gram_of(b_block), "ja")
    gram_c = lax.psum(gram_of(c_block), "ka")
    normal_a = gram_b * gram_c
    kr_a = (c_block[:, :, None] * b_block[:, None, :]).astype(jnp.bfloat16)
    partial_a = jnp.einsum("rkj,kij->ri", kr_a, tensor, preferred_element_type=jnp.float32)
    solved_a = solve_with(normal_a, partial_a)
    raw_a = lax.psum_scatter(
        arrange(solved_a, n_ja, n_ka), ("ja", "ka"), scatter_dimension=0, tiled=True
    )
    squares_a = lax.psum(jnp.sum(raw_a * raw_a, axis=1), ("ia", "ka"))
    local_a = scaled(raw_a, squares_a, total_i)
    pieces_a = lax.all_gather(local_a[None], ("ja", "ka"), axis=0, tiled=True)
    gathered_a = assemble(pieces_a, n_ja, n_ka)
    gram_a = lax.psum(gram_of(gathered_a), "ia")
    normal_b = gram_a * gram_c
    kr_b = (c_block[:, :, None] * gathered_a[:, None, :]).astype(jnp.bfloat16)
    partial_b = jnp.einsum("rki,kij->rj", kr_b, tensor, preferred_element_type=jnp.float32)
    solved_b = solve_with(normal_b, partial_b)
    raw_b = lax.psum_scatter(
        arrange(solved_b, n_ia, n_ka), ("ia", "ka"), scatter_dimension=0, tiled=True
    )
    squares_b = lax.psum(jnp.sum(raw_b * raw_b, axis=1), ("ja", "ka"))
    share_b = scaled(raw_b, squares_b, total_j)
    return (local_a, share_b)


MESH = pl.DeviceIdType.MESH
LANES = 128
SUBS = 8
NT = (((1,), (1,)), ((), ()))


def spread(src, dst, me, peers, send, recv):
    copies = []
    for step, peer in enumerate(peers, 1):
        copies.append(
            pltpu.make_async_remote_copy(
                src_ref=src,
                dst_ref=dst.at[me],
                send_sem=send.at[step],
                recv_sem=recv.at[step],
                device_id=peer,
                device_id_type=MESH,
            )
        )
    return copies


def ring(me, count):
    return [me] + [jnp.where(me + step >= count, me + step - count, me + step) for step in range(1, count)]


def stacked(pieces, rows):
    height, width = sum(p.shape[0] for p in pieces), pieces[0].shape[1]
    if rows > height:
        pieces = list(pieces) + [jnp.zeros((rows - height, width), pieces[0].dtype)]
    return jnp.concatenate(pieces, axis=0)


def wide_gram(block):
    other = stacked([block], LANES)
    return lax.dot_general(block, other, NT, precision=HIGH, preferred_element_type=jnp.float32)


def parts(values, rows):
    high = values.astype(jnp.bfloat16).astype(jnp.float32)
    rest = values - high
    middle = rest.astype(jnp.bfloat16).astype(jnp.float32)
    return stacked([high, middle, rest - middle], rows)


def folded(products, rank):
    total = products[0:rank] + products[rank : 2 * rank] + products[2 * rank : 3 * rank]
    return total + pltpu.roll(total, LANES - rank, 1) + pltpu.roll(total, LANES - 2 * rank, 1)


def masked(gram):
    lane = lax.broadcasted_iota(jnp.int32, gram.shape, 1)
    return jnp.where(lane < gram.shape[0], gram, 0.0)


def applied(solver, values):
    rank = solver.shape[0]
    s_parts = parts(solver, 3 * rank)
    high, middle, low = (s_parts[p * rank : (p + 1) * rank] for p in range(3))
    left = jnp.concatenate(
        [
            high + pltpu.roll(high, rank, 1) + pltpu.roll(high, 2 * rank, 1) + pltpu.roll(middle, 3 * rank, 1),
            middle + pltpu.roll(low, rank, 1),
        ],
        axis=1,
    ).astype(jnp.bfloat16)
    v_high, v_middle, v_low = (
        p.astype(jnp.bfloat16) for p in jnp.split(parts(values, 3 * rank), 3, axis=0)
    )
    blank = jnp.zeros_like(v_high)
    right = jnp.concatenate(
        [v_high, v_middle, v_low, v_high, v_middle, v_high, blank, blank], axis=0
    )
    return jnp.dot(left, right, preferred_element_type=jnp.float32)


def packed(gram):
    rank = gram.shape[0]
    tile = gram[0:SUBS]
    for q in range(1, rank // SUBS):
        tile = tile + pltpu.roll(gram[q * SUBS : (q + 1) * SUBS], q * rank, 1)
    return tile


def unpacked(tile, rank):
    lane = lax.broadcasted_iota(jnp.int32, (SUBS, LANES), 1)
    groups = []
    for q in range(rank // SUBS):
        moved = tile if q == 0 else pltpu.roll(tile, LANES - q * rank, 1)
        groups.append(jnp.where(lane < rank, moved, 0.0))
    return jnp.concatenate(groups, axis=0)


def inverse(normal):
    rank = normal.shape[0]
    blocks = [normal[q * SUBS : (q + 1) * SUBS] for q in range(rank // SUBS)]
    lane = lax.broadcasted_iota(jnp.int32, (SUBS, LANES), 1)
    sub = lax.broadcasted_iota(jnp.int32, (SUBS, LANES), 0)

    def column(block, index):
        return jnp.broadcast_to(block[:, index : index + 1], (SUBS, LANES))

    for q in range(rank // SUBS):
        first = q * SUBS
        cols = [[column(block, first + k) for k in range(SUBS)] for block in blocks]
        rows, inner = blocks[q], cols[q]
        for k in range(SUBS):
            col = inner[k]
            pivot = 1.0 / col[k : k + 1]
            row = jnp.where(lane[0:1] == first + k, 1.0, rows[k : k + 1]) * pivot
            rest = jnp.where(lane == first + k, 0.0, rows) - col * row
            rows = jnp.where(sub == k, row, rest)
            for m in range(k + 1, SUBS):
                entry = inner[m][k : k + 1] * pivot
                inner[m] = jnp.where(sub == k, entry, inner[m] - col * entry)
        inside = (lane >= first) & (lane < first + SUBS)
        for p in range(rank // SUBS):
            if p != q:
                total = jnp.where(inside, 0.0, blocks[p])
                for k in range(SUBS):
                    total = total - cols[p][k] * rows[k : k + 1]
                blocks[p] = total
        blocks[q] = rows
    return jnp.concatenate(blocks, axis=0)


def split(values):
    high = values.astype(jnp.bfloat16).astype(jnp.float32)
    return high, values - high


def kernel(
    n_ia, n_ja, total_i, total_j,
    t_ref, b_ref, c_ref, oa_ref, ob_ref,
    tv, ball, cin, cs, gb, pbuf, ra, ga, araw, gr, pb, rb, wsc, sq, rs, rf, prod,
    t_sem, in_sem, b_s, b_r, c_s, c_r, gb_s, gb_r, ra_s, ra_r, ga_s, ga_r,
    gr_s, gr_r, rb_s, rb_r, sq_s, sq_r, rf_s, rf_r,
):
    a = lax.axis_index("ia")
    j = lax.axis_index("ja")
    steps, width_i, width_j = tv.shape
    rank = n_ia * b_ref.shape[0]
    groups = rank // SUBS
    halves = n_ja // groups
    part_i = width_i // halves
    cuts_j = 2
    part_j = width_j // cuts_j
    piece_j = width_j // n_ia

    n_all = n_ia * n_ja
    mine = a * n_ja + j

    ring_a, ring_j = ring(a, n_ia), ring(j, n_ja)
    zero = jnp.int32(0)
    peers_ia = [(p, j, zero) for p in ring_a[1:]]
    peers_ja = [(a, q, zero) for q in ring_j[1:]]
    peers_all = [(p, q, zero) for q in reversed(ring_j) for p in ring_a][:-n_ia]
    peers_all = peers_all + peers_ia

    fetch_c = pltpu.make_async_copy(c_ref, cin, in_sem.at[0])
    fetch_b = pltpu.make_async_copy(b_ref, ball.at[a], in_sem.at[1])
    fetch_c.start()
    fetch_b.start()
    loads = []
    for h in range(halves):
        rows = pl.ds(h * part_i, part_i)
        load = pltpu.make_async_copy(t_ref.at[:, rows], tv.at[:, rows], t_sem.at[h])
        load.start()
        loads.append(load)

    barrier = pltpu.get_barrier_semaphore()
    for peer in peers_all:
        pl.semaphore_signal(barrier, inc=1, device_id=peer, device_id_type=MESH)
    fetch_c.wait()
    cs[mine] = jnp.zeros((1, LANES), jnp.float32)
    cs[mine, :, 0:steps] = cin[...]
    fetch_b.wait()
    pl.semaphore_wait(barrier, n_all - 1)

    sends = []

    def begin(copies):
        for copy in copies:
            copy.start()
        sends.extend(copies)
        return copies

    def arrived(copies):
        for copy in copies:
            copy.wait_recv()

    b_copies = begin(spread(ball.at[a], ball, a, peers_ia, b_s, b_r))
    c_copies = begin(spread(cs.at[mine], cs, mine, peers_all, c_s, c_r))
    arrived(b_copies)
    b_parts = parts(stacked([ball[s] for s in range(n_ia)], rank), LANES)
    weights = b_parts.T.astype(jnp.bfloat16)

    ra_copies = []
    for step in range(1, n_ja):
        peer = ring_j[step]
        ra_copies.append(
            pltpu.make_async_remote_copy(
                src_ref=pbuf.at[peer],
                dst_ref=ra.at[j],
                send_sem=ra_s.at[step],
                recv_sem=ra_r.at[step],
                device_id=(a, peer, zero),
                device_id_type=MESH,
            )
        )

    def product_a(h, k):
        return jnp.dot(
            tv[k, h * part_i : (h + 1) * part_i, :], weights, preferred_element_type=jnp.float32
        )

    loads[0].wait()
    for k in range(steps):
        prod[k] = product_a(0, k)
    gb[j] = packed(
        masked(
            folded(
                jnp.dot(b_parts.astype(jnp.bfloat16), weights, preferred_element_type=jnp.float32),
                rank,
            )
        )
    )
    gb_copies = begin(spread(gb.at[j], gb, j, peers_ja, gb_s, gb_r))
    arrived(c_copies)
    c_all = stacked([cs[s] for s in range(n_all)], rank)
    c_rows = stacked([c_all, c_all, c_all], LANES).T
    for h in range(halves):
        if h:
            loads[h].wait()
        total = jnp.zeros((part_i, LANES), jnp.float32)
        for k in range(steps):
            product = product_a(h, k) if h else prod[k]
            total = total + product * c_rows[k : k + 1, :]
        total = total.T
        total = total[0:rank] + total[rank : 2 * rank] + total[2 * rank : 3 * rank]
        for q in range(groups):
            pbuf[q * halves + h] = total[q * SUBS : (q + 1) * SUBS]
        for step in range(1, n_ja):
            @pl.when(lax.rem(ring_j[step], halves) == h)
            def _():
                ra_copies[step - 1].start()
    sends.extend(ra_copies)
    ra[j] = pbuf[j]
    gram_c = wide_gram(c_all)

    arrived(gb_copies)
    gram_b = unpacked(functools.reduce(jnp.add, [gb[s] for s in range(n_ja)]), rank)
    solve_a = inverse(gram_b * gram_c)

    arrived(ra_copies)
    ga[j] = functools.reduce(jnp.add, [ra[s] for s in range(n_ja)])
    ga_copies = begin(spread(ga.at[j], ga, j, peers_ja, ga_s, ga_r))
    c_cols = [c_all[:, k : k + 1] for k in range(steps)]
    arrived(ga_copies)
    summed = stacked(
        [
            jnp.concatenate([ga[q * halves + h] for h in range(halves)], axis=1)
            for q in range(groups)
        ],
        rank,
    )
    raw_a = applied(solve_a, summed)
    araw[...] = raw_a
    a_parts = parts(raw_a, LANES).astype(jnp.bfloat16)
    products = lax.dot_general(a_parts, a_parts, NT, preferred_element_type=jnp.float32)
    gr[a] = packed(masked(folded(products, rank)))
    gr_copies = begin(spread(gr.at[a], gr, a, peers_ia, gr_s, gr_r))

    rb_copies = []
    for step in range(1, n_ia):
        peer = ring_a[step]
        rb_copies.append(
            pltpu.make_async_remote_copy(
                src_ref=pb.at[peer],
                dst_ref=rb.at[a],
                send_sem=rb_s.at[step],
                recv_sem=rb_r.at[step],
                device_id=(peer, j, zero),
                device_id_type=MESH,
            )
        )
    pieces = []
    for k in range(steps):
        pieces.append(jnp.concatenate(split(raw_a * c_cols[k]), axis=0).astype(jnp.bfloat16))
    for h in range(cuts_j):
        total = jnp.zeros((2 * rank, part_j), jnp.float32)
        for k in range(steps):
            total = total + jnp.dot(
                pieces[k], tv[k, :, h * part_j : (h + 1) * part_j], preferred_element_type=jnp.float32
            )
        total = total[0:rank] + total[rank : 2 * rank]
        for m in range(n_ia // cuts_j):
            pb[h * (n_ia // cuts_j) + m] = total[:, m * piece_j : (m + 1) * piece_j]
        for step in range(1, n_ia):
            @pl.when(ring_a[step] // (n_ia // cuts_j) == h)
            def _():
                rb_copies[step - 1].start()
    sends.extend(rb_copies)
    rb[a] = pb[a]

    arrived(gr_copies)
    gram_a = unpacked(functools.reduce(jnp.add, [gr[s] for s in range(n_ia)]), rank)
    lane = lax.broadcasted_iota(jnp.int32, (rank, LANES), 1)
    sub = lax.broadcasted_iota(jnp.int32, (rank, LANES), 0)
    squares = jnp.where(lane == sub, gram_a, 0.0)
    scale_col = 1.0 / jnp.sqrt(jnp.sum(squares, axis=1, keepdims=True) / total_i + EPS)
    scale_row = 1.0 / jnp.sqrt(jnp.sum(squares, axis=0, keepdims=True) / total_i + EPS)
    solve_b = inverse(gram_a * scale_col * scale_row * gram_c) * scale_row
    new_a = araw[...] * scale_col
    for q in range(groups):
        araw[q * SUBS : (q + 1) * SUBS] = new_a[q * SUBS : (q + 1) * SUBS]
    height = rank // n_ja
    for p in range(n_ja):
        @pl.when(j == p)
        def _():
            oa_ref[...] = araw[p * height : (p + 1) * height, :]

    arrived(rb_copies)
    summed_b = functools.reduce(jnp.add, [rb[s] for s in range(n_ia)])
    raw_b = applied(solve_b, summed_b)
    sums = jnp.sum(raw_b * raw_b, axis=1, keepdims=True)
    sq[mine] = jnp.sum(jnp.where(lane == sub, sums, 0.0), axis=0, keepdims=True)
    for q in range(n_ia):
        rs[q] = raw_b[q * SUBS : (q + 1) * SUBS]
    rf[a] = rs[a]
    sq_copies = spread(sq.at[mine], sq, mine, peers_all, sq_s, sq_r)
    rf_copies = []
    for step in range(1, n_ia):
        peer = ring_a[step]
        rf_copies.append(
            pltpu.make_async_remote_copy(
                src_ref=rs.at[peer],
                dst_ref=rf.at[a],
                send_sem=rf_s.at[step],
                recv_sem=rf_r.at[step],
                device_id=(peer, j, zero),
                device_id_type=MESH,
            )
        )
    begin(rf_copies)
    begin(sq_copies)
    arrived(rf_copies)
    arrived(sq_copies)
    squares_b = functools.reduce(jnp.add, [sq[s] for s in range(n_all)])
    total_b = jnp.sum(jnp.where(lane == sub, squares_b, 0.0), axis=1, keepdims=True)
    scale_b = jnp.broadcast_to(1.0 / jnp.sqrt(total_b / total_j + EPS), (rank, LANES))
    for q in range(n_ia):
        wsc[q] = scale_b[q * SUBS : (q + 1) * SUBS]
    own = wsc[a]
    for q in range(n_ia):
        ob_ref[:, q * piece_j : (q + 1) * piece_j] = rf[q] * own

    for copy in sends:
        copy.wait_send()


def write_out(a_ref, b_ref, oa_ref, ob_ref, sems):
    copies = [
        pltpu.make_async_copy(a_ref, oa_ref, sems.at[0]),
        pltpu.make_async_copy(b_ref, ob_ref, sems.at[1]),
    ]
    for copy in copies:
        copy.start()
    for copy in copies:
        copy.wait()


def fused(tensor, factor_b, factor_c):
    n_ia = lax.axis_size("ia")
    n_ja = lax.axis_size("ja")
    steps, width_i, width_j = tensor.shape
    rows_b = factor_b.shape[0]
    rank = rows_b * n_ia
    halves = n_ja // (rank // SUBS)
    f32 = jnp.float32
    vmem = pltpu.VMEM
    dma = pltpu.SemaphoreType.DMA
    ja_sems = [dma((n_ja,)), dma((n_ja,))]
    ia_sems = [dma((n_ia,)), dma((n_ia,))]
    all_sems = [dma((n_ia * n_ja,)), dma((n_ia * n_ja,))]
    scratch = [
        vmem(tensor.shape, tensor.dtype),
        vmem((n_ia, rows_b, width_j), f32),
        vmem(factor_c.shape, f32),
        vmem((n_ia * n_ja, 1, LANES), f32),
        vmem((n_ja, SUBS, LANES), f32),
        vmem((n_ja, SUBS, width_i // halves), f32),
        vmem((n_ja, SUBS, width_i // halves), f32),
        vmem((n_ja, SUBS, width_i // halves), f32),
        vmem((rank, width_i), f32),
        vmem((n_ia, SUBS, LANES), f32),
        vmem((n_ia, rank, width_j // n_ia), f32),
        vmem((n_ia, rank, width_j // n_ia), f32),
        vmem((n_ia, SUBS, LANES), f32),
        vmem((n_ia * n_ja, 1, LANES), f32),
        vmem((n_ia, SUBS, width_j // n_ia), f32),
        vmem((n_ia, SUBS, width_j // n_ia), f32),
        vmem((steps, width_i // halves, LANES), f32),
        dma((halves,)),
        dma((2,)),
        *ia_sems, *all_sems, *ja_sems, *ja_sems, *ja_sems, *ia_sems, *ia_sems, *all_sems, *ia_sems,
    ]
    flops = 8 * rank * tensor.size
    results = pl.pallas_call(
        functools.partial(kernel, n_ia, n_ja, width_i * n_ia, width_j * n_ja),
        out_shape=(
            jax.ShapeDtypeStruct((rank // n_ja, width_i), f32),
            jax.ShapeDtypeStruct((rows_b, width_j), f32),
        ),
        in_specs=[
            pl.BlockSpec(memory_space=pltpu.HBM),
            pl.BlockSpec(memory_space=pltpu.HBM),
            pl.BlockSpec(memory_space=pltpu.HBM),
        ],
        out_specs=(pl.BlockSpec(memory_space=pltpu.VMEM), pl.BlockSpec(memory_space=pltpu.VMEM)),
        scratch_shapes=scratch,
        cost_estimate=pl.CostEstimate(flops=flops, bytes_accessed=2 * tensor.size, transcendentals=0),
        compiler_params=pltpu.CompilerParams(
            collective_id=0, has_side_effects=True, vmem_limit_bytes=56 * 2**20
        ),
    )(tensor, factor_b, factor_c)
    anywhere = pl.BlockSpec(memory_space=pl.ANY)
    return pl.pallas_call(
        write_out,
        out_shape=tuple(jax.ShapeDtypeStruct(r.shape, r.dtype) for r in results),
        in_specs=[anywhere, anywhere],
        out_specs=(anywhere, anywhere),
        scratch_shapes=[dma((2,))],
        compiler_params=pltpu.CompilerParams(vmem_limit_bytes=56 * 2**20),
    )(*results)


def fits(mesh):
    n_ia, n_ja, n_ka = (mesh.shape[name] for name in ("ia", "ja", "ka"))
    return n_ka == 1 and n_ia * SUBS == 32 and n_ja == 2 * n_ia


def solution(mesh):
    return jax.shard_map(
        fused if fits(mesh) else body,
        mesh=mesh,
        in_specs=(P("ka", "ia", "ja"), P("ia", ("ja", "ka")), P(("ia", "ja"), "ka")),
        out_specs=(P("ja", ("ia", "ka")), P("ia", ("ja", "ka"))),
        check_vma=False,
    )
```

```python
import functools

import jax
import jax.numpy as jnp
from jax import lax
from jax.experimental import pallas as pl
from jax.experimental.pallas import tpu as pltpu
from jax.sharding import PartitionSpec as P

EPS = 1e-06
HIGH = lax.Precision.HIGHEST


def gram_of(block):
    return jnp.dot(block, block.T, precision=HIGH, preferred_element_type=jnp.float32)


def solve_with(normal, rhs):
    lower = jnp.linalg.cholesky(normal)
    return jax.scipy.linalg.cho_solve((lower, True), rhs)


def arrange(partial_rows, rows_split, cols_split):
    rank, width = partial_rows.shape
    grid = partial_rows.reshape(rows_split, rank // rows_split, cols_split, width // cols_split)
    return grid.transpose(0, 2, 1, 3).reshape(rank * cols_split, width // cols_split)


def assemble(pieces, rows_split, cols_split):
    count, height, width = pieces.shape
    grid = pieces.reshape(rows_split, cols_split, height, width)
    return grid.transpose(0, 2, 1, 3).reshape(rows_split * height, cols_split * width)


def scaled(raw, squares, total):
    return raw / jnp.sqrt(squares / total + EPS)[:, None]


def body(tensor, factor_b, factor_c):
    n_ia = lax.axis_size("ia")
    n_ja = lax.axis_size("ja")
    n_ka = lax.axis_size("ka")
    total_i = tensor.shape[1] * n_ia
    total_j = tensor.shape[2] * n_ja
    c_block = lax.all_gather(factor_c, ("ia", "ja"), axis=0, tiled=True)
    pieces = lax.all_gather(factor_b[None], ("ia", "ka"), axis=0, tiled=True)
    b_block = assemble(pieces, n_ia, n_ka)
    gram_b = lax.psum(gram_of(b_block), "ja")
    gram_c = lax.psum(gram_of(c_block), "ka")
    normal_a = gram_b * gram_c
    kr_a = (c_block[:, :, None] * b_block[:, None, :]).astype(jnp.bfloat16)
    partial_a = jnp.einsum("rkj,kij->ri", kr_a, tensor, preferred_element_type=jnp.float32)
    solved_a = solve_with(normal_a, partial_a)
    raw_a = lax.psum_scatter(
        arrange(solved_a, n_ja, n_ka), ("ja", "ka"), scatter_dimension=0, tiled=True
    )
    squares_a = lax.psum(jnp.sum(raw_a * raw_a, axis=1), ("ia", "ka"))
    local_a = scaled(raw_a, squares_a, total_i)
    pieces_a = lax.all_gather(local_a[None], ("ja", "ka"), axis=0, tiled=True)
    gathered_a = assemble(pieces_a, n_ja, n_ka)
    gram_a = lax.psum(gram_of(gathered_a), "ia")
    normal_b = gram_a * gram_c
    kr_b = (c_block[:, :, None] * gathered_a[:, None, :]).astype(jnp.bfloat16)
    partial_b = jnp.einsum("rki,kij->rj", kr_b, tensor, preferred_element_type=jnp.float32)
    solved_b = solve_with(normal_b, partial_b)
    raw_b = lax.psum_scatter(
        arrange(solved_b, n_ia, n_ka), ("ia", "ka"), scatter_dimension=0, tiled=True
    )
    squares_b = lax.psum(jnp.sum(raw_b * raw_b, axis=1), ("ja", "ka"))
    share_b = scaled(raw_b, squares_b, total_j)
    return (local_a, share_b)


MESH = pl.DeviceIdType.MESH
LANES = 128
SUBS = 8
NT = (((1,), (1,)), ((), ()))


def spread(src, dst, me, peers, send, recv):
    copies = []
    for step, peer in enumerate(peers, 1):
        copies.append(
            pltpu.make_async_remote_copy(
                src_ref=src,
                dst_ref=dst.at[me],
                send_sem=send.at[step],
                recv_sem=recv.at[step],
                device_id=peer,
                device_id_type=MESH,
            )
        )
    return copies


def ring(me, count):
    return [me] + [jnp.where(me + step >= count, me + step - count, me + step) for step in range(1, count)]


def stacked(pieces, rows):
    height, width = sum(p.shape[0] for p in pieces), pieces[0].shape[1]
    if rows > height:
        pieces = list(pieces) + [jnp.zeros((rows - height, width), pieces[0].dtype)]
    return jnp.concatenate(pieces, axis=0)


def wide_gram(block):
    other = stacked([block], LANES)
    return lax.dot_general(block, other, NT, precision=HIGH, preferred_element_type=jnp.float32)


def parts(values, rows):
    high = values.astype(jnp.bfloat16).astype(jnp.float32)
    rest = values - high
    middle = rest.astype(jnp.bfloat16).astype(jnp.float32)
    return stacked([high, middle, rest - middle], rows)


def folded(products, rank):
    total = products[0:rank] + products[rank : 2 * rank] + products[2 * rank : 3 * rank]
    return total + pltpu.roll(total, LANES - rank, 1) + pltpu.roll(total, LANES - 2 * rank, 1)


def masked(gram):
    lane = lax.broadcasted_iota(jnp.int32, gram.shape, 1)
    return jnp.where(lane < gram.shape[0], gram, 0.0)


def applied(solver, values):
    rank = solver.shape[0]
    s_parts = parts(solver, 3 * rank)
    high, middle, low = (s_parts[p * rank : (p + 1) * rank] for p in range(3))
    left = jnp.concatenate(
        [
            high + pltpu.roll(high, rank, 1) + pltpu.roll(high, 2 * rank, 1) + pltpu.roll(middle, 3 * rank, 1),
            middle + pltpu.roll(low, rank, 1),
        ],
        axis=1,
    ).astype(jnp.bfloat16)
    v_high, v_middle, v_low = (
        p.astype(jnp.bfloat16) for p in jnp.split(parts(values, 3 * rank), 3, axis=0)
    )
    blank = jnp.zeros_like(v_high)
    right = jnp.concatenate(
        [v_high, v_middle, v_low, v_high, v_middle, v_high, blank, blank], axis=0
    )
    return jnp.dot(left, right, preferred_element_type=jnp.float32)


def packed(gram):
    rank = gram.shape[0]
    tile = gram[0:SUBS]
    for q in range(1, rank // SUBS):
        tile = tile + pltpu.roll(gram[q * SUBS : (q + 1) * SUBS], q * rank, 1)
    return tile


def unpacked(tile, rank):
    lane = lax.broadcasted_iota(jnp.int32, (SUBS, LANES), 1)
    groups = []
    for q in range(rank // SUBS):
        moved = tile if q == 0 else pltpu.roll(tile, LANES - q * rank, 1)
        groups.append(jnp.where(lane < rank, moved, 0.0))
    return jnp.concatenate(groups, axis=0)


def inverse(normal):
    rank = normal.shape[0]
    blocks = [normal[q * SUBS : (q + 1) * SUBS] for q in range(rank // SUBS)]
    lane = lax.broadcasted_iota(jnp.int32, (SUBS, LANES), 1)
    sub = lax.broadcasted_iota(jnp.int32, (SUBS, LANES), 0)

    def column(block, index):
        return jnp.broadcast_to(block[:, index : index + 1], (SUBS, LANES))

    for q in range(rank // SUBS):
        first = q * SUBS
        cols = [[column(block, first + k) for k in range(SUBS)] for block in blocks]
        rows, inner = blocks[q], cols[q]
        for k in range(SUBS):
            col = inner[k]
            pivot = 1.0 / col[k : k + 1]
            row = jnp.where(lane[0:1] == first + k, 1.0, rows[k : k + 1]) * pivot
            rest = jnp.where(lane == first + k, 0.0, rows) - col * row
            rows = jnp.where(sub == k, row, rest)
            for m in range(k + 1, SUBS):
                entry = inner[m][k : k + 1] * pivot
                inner[m] = jnp.where(sub == k, entry, inner[m] - col * entry)
        inside = (lane >= first) & (lane < first + SUBS)
        for p in range(rank // SUBS):
            if p != q:
                total = jnp.where(inside, 0.0, blocks[p])
                for k in range(SUBS):
                    total = total - cols[p][k] * rows[k : k + 1]
                blocks[p] = total
        blocks[q] = rows
    return jnp.concatenate(blocks, axis=0)


def split(values):
    high = values.astype(jnp.bfloat16).astype(jnp.float32)
    return high, values - high


def kernel(
    n_ia, n_ja, total_i, total_j,
    t_ref, b_ref, c_ref, oa_ref, ob_ref,
    tv, ball, cin, cs, gb, pbuf, ra, ga, araw, gr, pb, rb, wsc, sq, rs, rf, prod,
    t_sem, in_sem, b_s, b_r, c_s, c_r, gb_s, gb_r, ra_s, ra_r, ga_s, ga_r,
    gr_s, gr_r, rb_s, rb_r, sq_s, sq_r, rf_s, rf_r,
):
    a = lax.axis_index("ia")
    j = lax.axis_index("ja")
    steps, width_i, width_j = tv.shape
    rank = n_ia * b_ref.shape[0]
    groups = rank // SUBS
    halves = n_ja // groups
    part_i = width_i // halves
    piece_j = width_j // n_ia

    n_all = n_ia * n_ja
    mine = a * n_ja + j

    ring_a, ring_j = ring(a, n_ia), ring(j, n_ja)
    zero = jnp.int32(0)
    peers_ia = [(p, j, zero) for p in ring_a[1:]]
    peers_ja = [(a, q, zero) for q in ring_j[1:]]
    peers_all = [(p, q, zero) for q in reversed(ring_j) for p in ring_a][:-n_ia]
    peers_all = peers_all + peers_ia

    fetch_c = pltpu.make_async_copy(c_ref, cin, in_sem.at[0])
    fetch_b = pltpu.make_async_copy(b_ref, ball.at[a], in_sem.at[1])
    fetch_c.start()
    fetch_b.start()
    loads = []
    for k in range(steps):
        load = pltpu.make_async_copy(t_ref.at[k], tv.at[k], t_sem.at[k])
        load.start()
        loads.append(load)

    barrier = pltpu.get_barrier_semaphore()
    for peer in peers_all:
        pl.semaphore_signal(barrier, inc=1, device_id=peer, device_id_type=MESH)
    fetch_c.wait()
    cs[mine] = jnp.zeros((1, LANES), jnp.float32)
    cs[mine, :, 0:steps] = cin[...]
    fetch_b.wait()
    pl.semaphore_wait(barrier, n_all - 1)

    sends = []

    def begin(copies):
        for copy in copies:
            copy.start()
        sends.extend(copies)
        return copies

    def arrived(copies):
        for copy in copies:
            copy.wait_recv()

    b_copies = begin(spread(ball.at[a], ball, a, peers_ia, b_s, b_r))
    c_copies = begin(spread(cs.at[mine], cs, mine, peers_all, c_s, c_r))
    arrived(b_copies)
    b_parts = parts(stacked([ball[s] for s in range(n_ia)], rank), LANES)
    weights = b_parts.T.astype(jnp.bfloat16)

    ra_copies = []
    for step in range(1, n_ja):
        peer = ring_j[step]
        ra_copies.append(
            pltpu.make_async_remote_copy(
                src_ref=pbuf.at[peer],
                dst_ref=ra.at[j],
                send_sem=ra_s.at[step],
                recv_sem=ra_r.at[step],
                device_id=(a, peer, zero),
                device_id_type=MESH,
            )
        )

    for load in loads:
        load.wait()
    prod[...] = jnp.dot(
        tv[...].reshape(steps * width_i, width_j), weights, preferred_element_type=jnp.float32
    ).reshape(prod.shape)
    gb[j] = packed(
        masked(
            folded(
                jnp.dot(b_parts.astype(jnp.bfloat16), weights, preferred_element_type=jnp.float32),
                rank,
            )
        )
    )
    gb_copies = begin(spread(gb.at[j], gb, j, peers_ja, gb_s, gb_r))
    arrived(c_copies)
    c_all = stacked([cs[s] for s in range(n_all)], rank)
    c_rows = stacked([c_all, c_all, c_all], LANES).T
    for h in range(halves):
        total = jnp.zeros((part_i, LANES), jnp.float32)
        for k in range(steps):
            total = total + prod[k, h * part_i : (h + 1) * part_i, :] * c_rows[k : k + 1, :]
        total = total.T
        total = total[0:rank] + total[rank : 2 * rank] + total[2 * rank : 3 * rank]
        for q in range(groups):
            pbuf[q * halves + h] = total[q * SUBS : (q + 1) * SUBS]
        for step in range(1, n_ja):
            @pl.when(lax.rem(ring_j[step], halves) == h)
            def _():
                ra_copies[step - 1].start()
    sends.extend(ra_copies)
    ra[j] = pbuf[j]
    gram_c = wide_gram(c_all)

    arrived(gb_copies)
    gram_b = unpacked(functools.reduce(jnp.add, [gb[s] for s in range(n_ja)]), rank)
    solve_a = inverse(gram_b * gram_c)

    arrived(ra_copies)
    ga[j] = functools.reduce(jnp.add, [ra[s] for s in range(n_ja)])
    ga_copies = begin(spread(ga.at[j], ga, j, peers_ja, ga_s, ga_r))
    c_cols = [c_all[:, k : k + 1] for k in range(steps)]
    arrived(ga_copies)
    summed = stacked(
        [
            jnp.concatenate([ga[q * halves + h] for h in range(halves)], axis=1)
            for q in range(groups)
        ],
        rank,
    )
    raw_a = applied(solve_a, summed)
    araw[...] = raw_a
    a_parts = parts(raw_a, LANES).astype(jnp.bfloat16)
    products = lax.dot_general(a_parts, a_parts, NT, preferred_element_type=jnp.float32)
    gr[a] = packed(masked(folded(products, rank)))
    gr_copies = begin(spread(gr.at[a], gr, a, peers_ia, gr_s, gr_r))

    rb_copies = []
    for step in range(1, n_ia):
        peer = ring_a[step]
        rb_copies.append(
            pltpu.make_async_remote_copy(
                src_ref=pb.at[peer],
                dst_ref=rb.at[a],
                send_sem=rb_s.at[step],
                recv_sem=rb_r.at[step],
                device_id=(peer, j, zero),
                device_id_type=MESH,
            )
        )
    pieces = []
    for k in range(steps):
        pieces.append(jnp.concatenate(split(raw_a * c_cols[k]), axis=0).astype(jnp.bfloat16))
    total = jnp.dot(
        jnp.concatenate(pieces, axis=1),
        tv[...].reshape(steps * width_i, width_j),
        preferred_element_type=jnp.float32,
    )
    total = total[0:rank] + total[rank : 2 * rank]
    for p in range(n_ia):
        pb[p] = total[:, p * piece_j : (p + 1) * piece_j]
    for copy in rb_copies:
        copy.start()
    sends.extend(rb_copies)
    rb[a] = pb[a]

    arrived(gr_copies)
    gram_a = unpacked(functools.reduce(jnp.add, [gr[s] for s in range(n_ia)]), rank)
    lane = lax.broadcasted_iota(jnp.int32, (rank, LANES), 1)
    sub = lax.broadcasted_iota(jnp.int32, (rank, LANES), 0)
    squares = jnp.where(lane == sub, gram_a, 0.0)
    scale_col = 1.0 / jnp.sqrt(jnp.sum(squares, axis=1, keepdims=True) / total_i + EPS)
    scale_row = 1.0 / jnp.sqrt(jnp.sum(squares, axis=0, keepdims=True) / total_i + EPS)
    solve_b = inverse(gram_a * scale_col * scale_row * gram_c) * scale_row
    new_a = araw[...] * scale_col
    for q in range(groups):
        araw[q * SUBS : (q + 1) * SUBS] = new_a[q * SUBS : (q + 1) * SUBS]
    height = rank // n_ja
    for p in range(n_ja):
        @pl.when(j == p)
        def _():
            oa_ref[...] = araw[p * height : (p + 1) * height, :]

    arrived(rb_copies)
    summed_b = functools.reduce(jnp.add, [rb[s] for s in range(n_ia)])
    raw_b = applied(solve_b, summed_b)
    sums = jnp.sum(raw_b * raw_b, axis=1, keepdims=True)
    sq[mine] = jnp.sum(jnp.where(lane == sub, sums, 0.0), axis=0, keepdims=True)
    for q in range(n_ia):
        rs[q] = raw_b[q * SUBS : (q + 1) * SUBS]
    rf[a] = rs[a]
    sq_copies = spread(sq.at[mine], sq, mine, peers_all, sq_s, sq_r)
    rf_copies = []
    for step in range(1, n_ia):
        peer = ring_a[step]
        rf_copies.append(
            pltpu.make_async_remote_copy(
                src_ref=rs.at[peer],
                dst_ref=rf.at[a],
                send_sem=rf_s.at[step],
                recv_sem=rf_r.at[step],
                device_id=(peer, j, zero),
                device_id_type=MESH,
            )
        )
    begin(rf_copies)
    begin(sq_copies)
    arrived(rf_copies)
    arrived(sq_copies)
    squares_b = functools.reduce(jnp.add, [sq[s] for s in range(n_all)])
    total_b = jnp.sum(jnp.where(lane == sub, squares_b, 0.0), axis=1, keepdims=True)
    scale_b = jnp.broadcast_to(1.0 / jnp.sqrt(total_b / total_j + EPS), (rank, LANES))
    for q in range(n_ia):
        wsc[q] = scale_b[q * SUBS : (q + 1) * SUBS]
    own = wsc[a]
    for q in range(n_ia):
        ob_ref[:, q * piece_j : (q + 1) * piece_j] = rf[q] * own

    for copy in sends:
        copy.wait_send()


def write_out(a_ref, b_ref, oa_ref, ob_ref, sems):
    copies = [
        pltpu.make_async_copy(a_ref, oa_ref, sems.at[0]),
        pltpu.make_async_copy(b_ref, ob_ref, sems.at[1]),
    ]
    for copy in copies:
        copy.start()
    for copy in copies:
        copy.wait()


def fused(tensor, factor_b, factor_c):
    n_ia = lax.axis_size("ia")
    n_ja = lax.axis_size("ja")
    steps, width_i, width_j = tensor.shape
    rows_b = factor_b.shape[0]
    rank = rows_b * n_ia
    halves = n_ja // (rank // SUBS)
    f32 = jnp.float32
    vmem = pltpu.VMEM
    dma = pltpu.SemaphoreType.DMA
    ja_sems = [dma((n_ja,)), dma((n_ja,))]
    ia_sems = [dma((n_ia,)), dma((n_ia,))]
    all_sems = [dma((n_ia * n_ja,)), dma((n_ia * n_ja,))]
    scratch = [
        vmem(tensor.shape, tensor.dtype),
        vmem((n_ia, rows_b, width_j), f32),
        vmem(factor_c.shape, f32),
        vmem((n_ia * n_ja, 1, LANES), f32),
        vmem((n_ja, SUBS, LANES), f32),
        vmem((n_ja, SUBS, width_i // halves), f32),
        vmem((n_ja, SUBS, width_i // halves), f32),
        vmem((n_ja, SUBS, width_i // halves), f32),
        vmem((rank, width_i), f32),
        vmem((n_ia, SUBS, LANES), f32),
        vmem((n_ia, rank, width_j // n_ia), f32),
        vmem((n_ia, rank, width_j // n_ia), f32),
        vmem((n_ia, SUBS, LANES), f32),
        vmem((n_ia * n_ja, 1, LANES), f32),
        vmem((n_ia, SUBS, width_j // n_ia), f32),
        vmem((n_ia, SUBS, width_j // n_ia), f32),
        vmem((steps, width_i, LANES), f32),
        dma((steps,)),
        dma((2,)),
        *ia_sems, *all_sems, *ja_sems, *ja_sems, *ja_sems, *ia_sems, *ia_sems, *all_sems, *ia_sems,
    ]
    flops = 8 * rank * tensor.size
    results = pl.pallas_call(
        functools.partial(kernel, n_ia, n_ja, width_i * n_ia, width_j * n_ja),
        out_shape=(
            jax.ShapeDtypeStruct((rank // n_ja, width_i), f32),
            jax.ShapeDtypeStruct((rows_b, width_j), f32),
        ),
        in_specs=[
            pl.BlockSpec(memory_space=pltpu.HBM),
            pl.BlockSpec(memory_space=pltpu.HBM),
            pl.BlockSpec(memory_space=pltpu.HBM),
        ],
        out_specs=(pl.BlockSpec(memory_space=pltpu.VMEM), pl.BlockSpec(memory_space=pltpu.VMEM)),
        scratch_shapes=scratch,
        cost_estimate=pl.CostEstimate(flops=flops, bytes_accessed=2 * tensor.size, transcendentals=0),
        compiler_params=pltpu.CompilerParams(
            collective_id=0, has_side_effects=True, vmem_limit_bytes=56 * 2**20
        ),
    )(tensor, factor_b, factor_c)
    anywhere = pl.BlockSpec(memory_space=pl.ANY)
    return pl.pallas_call(
        write_out,
        out_shape=tuple(jax.ShapeDtypeStruct(r.shape, r.dtype) for r in results),
        in_specs=[anywhere, anywhere],
        out_specs=(anywhere, anywhere),
        scratch_shapes=[dma((2,))],
        compiler_params=pltpu.CompilerParams(vmem_limit_bytes=56 * 2**20),
    )(*results)


def fits(mesh):
    n_ia, n_ja, n_ka = (mesh.shape[name] for name in ("ia", "ja", "ka"))
    return n_ka == 1 and n_ia * SUBS == 32 and n_ja == 2 * n_ia


def solution(mesh):
    return jax.shard_map(
        fused if fits(mesh) else body,
        mesh=mesh,
        in_specs=(P("ka", "ia", "ja"), P("ia", ("ja", "ka")), P(("ia", "ja"), "ka")),
        out_specs=(P("ja", ("ia", "ka")), P("ia", ("ja", "ka"))),
        check_vma=False,
    )
```

```python
import functools

import jax
import jax.numpy as jnp
from jax import lax
from jax.experimental import pallas as pl
from jax.experimental.pallas import tpu as pltpu
from jax.sharding import PartitionSpec as P

EPS = 1e-06
HIGH = lax.Precision.HIGHEST


def gram_of(block):
    return jnp.dot(block, block.T, precision=HIGH, preferred_element_type=jnp.float32)


def solve_with(normal, rhs):
    lower = jnp.linalg.cholesky(normal)
    return jax.scipy.linalg.cho_solve((lower, True), rhs)


def arrange(partial_rows, rows_split, cols_split):
    rank, width = partial_rows.shape
    grid = partial_rows.reshape(rows_split, rank // rows_split, cols_split, width // cols_split)
    return grid.transpose(0, 2, 1, 3).reshape(rank * cols_split, width // cols_split)


def assemble(pieces, rows_split, cols_split):
    count, height, width = pieces.shape
    grid = pieces.reshape(rows_split, cols_split, height, width)
    return grid.transpose(0, 2, 1, 3).reshape(rows_split * height, cols_split * width)


def scaled(raw, squares, total):
    return raw / jnp.sqrt(squares / total + EPS)[:, None]


def body(tensor, factor_b, factor_c):
    n_ia = lax.axis_size("ia")
    n_ja = lax.axis_size("ja")
    n_ka = lax.axis_size("ka")
    total_i = tensor.shape[1] * n_ia
    total_j = tensor.shape[2] * n_ja
    c_block = lax.all_gather(factor_c, ("ia", "ja"), axis=0, tiled=True)
    pieces = lax.all_gather(factor_b[None], ("ia", "ka"), axis=0, tiled=True)
    b_block = assemble(pieces, n_ia, n_ka)
    gram_b = lax.psum(gram_of(b_block), "ja")
    gram_c = lax.psum(gram_of(c_block), "ka")
    normal_a = gram_b * gram_c
    kr_a = (c_block[:, :, None] * b_block[:, None, :]).astype(jnp.bfloat16)
    partial_a = jnp.einsum("rkj,kij->ri", kr_a, tensor, preferred_element_type=jnp.float32)
    solved_a = solve_with(normal_a, partial_a)
    raw_a = lax.psum_scatter(
        arrange(solved_a, n_ja, n_ka), ("ja", "ka"), scatter_dimension=0, tiled=True
    )
    squares_a = lax.psum(jnp.sum(raw_a * raw_a, axis=1), ("ia", "ka"))
    local_a = scaled(raw_a, squares_a, total_i)
    pieces_a = lax.all_gather(local_a[None], ("ja", "ka"), axis=0, tiled=True)
    gathered_a = assemble(pieces_a, n_ja, n_ka)
    gram_a = lax.psum(gram_of(gathered_a), "ia")
    normal_b = gram_a * gram_c
    kr_b = (c_block[:, :, None] * gathered_a[:, None, :]).astype(jnp.bfloat16)
    partial_b = jnp.einsum("rki,kij->rj", kr_b, tensor, preferred_element_type=jnp.float32)
    solved_b = solve_with(normal_b, partial_b)
    raw_b = lax.psum_scatter(
        arrange(solved_b, n_ia, n_ka), ("ia", "ka"), scatter_dimension=0, tiled=True
    )
    squares_b = lax.psum(jnp.sum(raw_b * raw_b, axis=1), ("ja", "ka"))
    share_b = scaled(raw_b, squares_b, total_j)
    return (local_a, share_b)


MESH = pl.DeviceIdType.MESH
LANES = 128
SUBS = 8
NT = (((1,), (1,)), ((), ()))


def spread(src, dst, me, peers, send, recv):
    copies = []
    for step, peer in enumerate(peers, 1):
        copies.append(
            pltpu.make_async_remote_copy(
                src_ref=src,
                dst_ref=dst.at[me],
                send_sem=send.at[step],
                recv_sem=recv.at[step],
                device_id=peer,
                device_id_type=MESH,
            )
        )
    return copies


def ring(me, count):
    return [me] + [jnp.where(me + step >= count, me + step - count, me + step) for step in range(1, count)]


def stacked(pieces, rows):
    height, width = sum(p.shape[0] for p in pieces), pieces[0].shape[1]
    if rows > height:
        pieces = list(pieces) + [jnp.zeros((rows - height, width), pieces[0].dtype)]
    return jnp.concatenate(pieces, axis=0)


def wide_gram(block):
    other = stacked([block], LANES)
    return lax.dot_general(block, other, NT, precision=HIGH, preferred_element_type=jnp.float32)


def parts(values, rows):
    high = values.astype(jnp.bfloat16).astype(jnp.float32)
    rest = values - high
    middle = rest.astype(jnp.bfloat16).astype(jnp.float32)
    return stacked([high, middle, rest - middle], rows)


def folded(products, rank):
    total = products[0:rank] + products[rank : 2 * rank] + products[2 * rank : 3 * rank]
    return total + pltpu.roll(total, LANES - rank, 1) + pltpu.roll(total, LANES - 2 * rank, 1)


def masked(gram):
    lane = lax.broadcasted_iota(jnp.int32, gram.shape, 1)
    return jnp.where(lane < gram.shape[0], gram, 0.0)


def applied(solver, values):
    rank = solver.shape[0]
    s_parts = parts(solver, 3 * rank)
    high, middle, low = (s_parts[p * rank : (p + 1) * rank] for p in range(3))
    left = jnp.concatenate(
        [
            high + pltpu.roll(high, rank, 1) + pltpu.roll(high, 2 * rank, 1) + pltpu.roll(middle, 3 * rank, 1),
            middle + pltpu.roll(low, rank, 1),
        ],
        axis=1,
    ).astype(jnp.bfloat16)
    v_high, v_middle, v_low = (
        p.astype(jnp.bfloat16) for p in jnp.split(parts(values, 3 * rank), 3, axis=0)
    )
    blank = jnp.zeros_like(v_high)
    right = jnp.concatenate(
        [v_high, v_middle, v_low, v_high, v_middle, v_high, blank, blank], axis=0
    )
    return jnp.dot(left, right, preferred_element_type=jnp.float32)


def packed(gram):
    rank = gram.shape[0]
    tile = gram[0:SUBS]
    for q in range(1, rank // SUBS):
        tile = tile + pltpu.roll(gram[q * SUBS : (q + 1) * SUBS], q * rank, 1)
    return tile


def unpacked(tile, rank):
    lane = lax.broadcasted_iota(jnp.int32, (SUBS, LANES), 1)
    groups = []
    for q in range(rank // SUBS):
        moved = tile if q == 0 else pltpu.roll(tile, LANES - q * rank, 1)
        groups.append(jnp.where(lane < rank, moved, 0.0))
    return jnp.concatenate(groups, axis=0)


def inverse(normal):
    rank = normal.shape[0]
    blocks = [normal[q * SUBS : (q + 1) * SUBS] for q in range(rank // SUBS)]
    lane = lax.broadcasted_iota(jnp.int32, (SUBS, LANES), 1)
    sub = lax.broadcasted_iota(jnp.int32, (SUBS, LANES), 0)

    def column(block, index):
        return jnp.broadcast_to(block[:, index : index + 1], (SUBS, LANES))

    for q in range(rank // SUBS):
        first = q * SUBS
        cols = [[column(block, first + k) for k in range(SUBS)] for block in blocks]
        rows, inner = blocks[q], cols[q]
        for k in range(SUBS):
            col = inner[k]
            pivot = 1.0 / col[k : k + 1]
            row = jnp.where(lane[0:1] == first + k, 1.0, rows[k : k + 1]) * pivot
            rest = jnp.where(lane == first + k, 0.0, rows) - col * row
            rows = jnp.where(sub == k, row, rest)
            for m in range(k + 1, SUBS):
                entry = inner[m][k : k + 1] * pivot
                inner[m] = jnp.where(sub == k, entry, inner[m] - col * entry)
        inside = (lane >= first) & (lane < first + SUBS)
        for p in range(rank // SUBS):
            if p != q:
                total = jnp.where(inside, 0.0, blocks[p])
                for k in range(SUBS):
                    total = total - cols[p][k] * rows[k : k + 1]
                blocks[p] = total
        blocks[q] = rows
    return jnp.concatenate(blocks, axis=0)


def split(values):
    high = values.astype(jnp.bfloat16).astype(jnp.float32)
    return high, values - high


def kernel(
    n_ia, n_ja, total_i, total_j,
    t_ref, b_ref, c_ref, oa_ref, ob_ref,
    tv, ball, cin, cs, gb, pbuf, ra, ga, araw, gr, pb, rb, wsc, sq, rs, rf, prod,
    t_sem, in_sem, b_s, b_r, c_s, c_r, gb_s, gb_r, ra_s, ra_r, ga_s, ga_r,
    gr_s, gr_r, rb_s, rb_r, sq_s, sq_r, rf_s, rf_r,
):
    a = lax.axis_index("ia")
    j = lax.axis_index("ja")
    steps, width_i, width_j = tv.shape
    rank = n_ia * b_ref.shape[0]
    groups = rank // SUBS
    halves = n_ja // groups
    part_i = width_i // halves
    cuts_j = 2
    part_j = width_j // cuts_j
    piece_j = width_j // n_ia

    n_all = n_ia * n_ja
    mine = a * n_ja + j

    ring_a, ring_j = ring(a, n_ia), ring(j, n_ja)
    zero = jnp.int32(0)
    peers_ia = [(p, j, zero) for p in ring_a[1:]]
    peers_ja = [(a, q, zero) for q in ring_j[1:]]
    peers_all = [(p, q, zero) for q in reversed(ring_j) for p in ring_a][:-n_ia]
    peers_all = peers_all + peers_ia

    fetch_c = pltpu.make_async_copy(c_ref, cin, in_sem.at[0])
    fetch_b = pltpu.make_async_copy(b_ref, ball.at[a], in_sem.at[1])
    fetch_c.start()
    fetch_b.start()
    loads = []
    for h in range(halves):
        rows = pl.ds(h * part_i, part_i)
        load = pltpu.make_async_copy(t_ref.at[:, rows], tv.at[:, rows], t_sem.at[h])
        load.start()
        loads.append(load)

    barrier = pltpu.get_barrier_semaphore()
    for peer in peers_all:
        pl.semaphore_signal(barrier, inc=1, device_id=peer, device_id_type=MESH)
    fetch_c.wait()
    cs[mine] = jnp.zeros((1, LANES), jnp.float32)
    cs[mine, :, 0:steps] = cin[...]
    fetch_b.wait()
    pl.semaphore_wait(barrier, n_all - 1)

    sends = []

    def begin(copies):
        for copy in copies:
            copy.start()
        sends.extend(copies)
        return copies

    def arrived(copies):
        for copy in copies:
            copy.wait_recv()

    b_copies = begin(spread(ball.at[a], ball, a, peers_ia, b_s, b_r))
    c_copies = begin(spread(cs.at[mine], cs, mine, peers_all, c_s, c_r))
    arrived(b_copies)
    b_parts = parts(stacked([ball[s] for s in range(n_ia)], rank), LANES)
    weights = b_parts.T.astype(jnp.bfloat16)

    ra_copies = []
    for step in range(1, n_ja):
        peer = ring_j[step]
        ra_copies.append(
            pltpu.make_async_remote_copy(
                src_ref=pbuf.at[peer],
                dst_ref=ra.at[j],
                send_sem=ra_s.at[step],
                recv_sem=ra_r.at[step],
                device_id=(a, peer, zero),
                device_id_type=MESH,
            )
        )

    def product_a(h, k):
        return jnp.dot(
            tv[k, h * part_i : (h + 1) * part_i, :], weights, preferred_element_type=jnp.float32
        )

    loads[0].wait()
    for k in range(steps):
        prod[k] = product_a(0, k)
    gb[j] = packed(
        masked(
            folded(
                jnp.dot(b_parts.astype(jnp.bfloat16), weights, preferred_element_type=jnp.float32),
                rank,
            )
        )
    )
    gb_copies = begin(spread(gb.at[j], gb, j, peers_ja, gb_s, gb_r))
    arrived(c_copies)
    c_all = stacked([cs[s] for s in range(n_all)], rank)
    c_rows = stacked([c_all, c_all, c_all], LANES).T
    for h in range(halves):
        if h:
            loads[h].wait()
        total = jnp.zeros((part_i, LANES), jnp.float32)
        for k in range(steps):
            product = product_a(h, k) if h else prod[k]
            total = total + product * c_rows[k : k + 1, :]
        total = total.T
        total = total[0:rank] + total[rank : 2 * rank] + total[2 * rank : 3 * rank]
        for q in range(groups):
            pbuf[q * halves + h] = total[q * SUBS : (q + 1) * SUBS]
        for step in range(1, n_ja):
            @pl.when(lax.rem(ring_j[step], halves) == h)
            def _():
                ra_copies[step - 1].start()
    sends.extend(ra_copies)
    ra[j] = pbuf[j]
    gram_c = wide_gram(c_all)

    arrived(gb_copies)
    gram_b = unpacked(functools.reduce(jnp.add, [gb[s] for s in range(n_ja)]), rank)
    solve_a = inverse(gram_b * gram_c)

    arrived(ra_copies)
    ga[j] = functools.reduce(jnp.add, [ra[s] for s in range(n_ja)])
    ga_copies = begin(spread(ga.at[j], ga, j, peers_ja, ga_s, ga_r))
    c_cols = [c_all[:, k : k + 1] for k in range(steps)]

    rb_copies = []
    for step in range(1, n_ia):
        peer = ring_a[step]
        rb_copies.append(
            pltpu.make_async_remote_copy(
                src_ref=pb.at[peer],
                dst_ref=rb.at[a],
                send_sem=rb_s.at[step],
                recv_sem=rb_r.at[step],
                device_id=(peer, j, zero),
                device_id_type=MESH,
            )
        )

    total = None
    products = None
    for h in range(halves):
        for step in range(1, n_ja):
            @pl.when(lax.rem(ring_j[n_ja - step], halves) == h)
            def _():
                ga_copies[step - 1].wait_recv()
        summed = stacked([ga[q * halves + h] for q in range(groups)], rank)
        raw_a = applied(solve_a, summed)
        cut_i = slice(h * part_i, (h + 1) * part_i)
        araw[:, cut_i] = raw_a
        a_parts = parts(raw_a, LANES).astype(jnp.bfloat16)
        block = lax.dot_general(a_parts, a_parts, NT, preferred_element_type=jnp.float32)
        products = block if products is None else products + block
        if h == halves - 1:
            gr[a] = packed(masked(folded(products, rank)))
            gr_copies = begin(spread(gr.at[a], gr, a, peers_ia, gr_s, gr_r))
        pieces = [
            jnp.concatenate(split(raw_a * c_cols[k]), axis=0).astype(jnp.bfloat16)
            for k in range(steps)
        ]
        if h < halves - 1:
            for k in range(steps):
                block = jnp.dot(pieces[k], tv[k, cut_i, :], preferred_element_type=jnp.float32)
                total = block if total is None else total + block
    for m in range(cuts_j):
        cut_j = slice(m * part_j, (m + 1) * part_j)
        done = total[:, cut_j]
        for k in range(steps):
            done = done + jnp.dot(
                pieces[k], tv[k, cut_i, cut_j], preferred_element_type=jnp.float32
            )
        done = done[0:rank] + done[rank : 2 * rank]
        per_cut = n_ia // cuts_j
        for p in range(per_cut):
            pb[m * per_cut + p] = done[:, p * piece_j : (p + 1) * piece_j]
        for step in range(1, n_ia):
            @pl.when(ring_a[step] // per_cut == m)
            def _():
                rb_copies[step - 1].start()
    sends.extend(rb_copies)
    rb[a] = pb[a]

    arrived(gr_copies)
    gram_a = unpacked(functools.reduce(jnp.add, [gr[s] for s in range(n_ia)]), rank)
    lane = lax.broadcasted_iota(jnp.int32, (rank, LANES), 1)
    sub = lax.broadcasted_iota(jnp.int32, (rank, LANES), 0)
    squares = jnp.where(lane == sub, gram_a, 0.0)
    scale_col = 1.0 / jnp.sqrt(jnp.sum(squares, axis=1, keepdims=True) / total_i + EPS)
    scale_row = 1.0 / jnp.sqrt(jnp.sum(squares, axis=0, keepdims=True) / total_i + EPS)
    solve_b = inverse(gram_a * scale_col * scale_row * gram_c) * scale_row
    new_a = araw[...] * scale_col
    for q in range(groups):
        araw[q * SUBS : (q + 1) * SUBS] = new_a[q * SUBS : (q + 1) * SUBS]
    height = rank // n_ja
    for p in range(n_ja):
        @pl.when(j == p)
        def _():
            oa_ref[...] = araw[p * height : (p + 1) * height, :]

    arrived(rb_copies)
    summed_b = functools.reduce(jnp.add, [rb[s] for s in range(n_ia)])
    raw_b = applied(solve_b, summed_b)
    sums = jnp.sum(raw_b * raw_b, axis=1, keepdims=True)
    sq[mine] = jnp.sum(jnp.where(lane == sub, sums, 0.0), axis=0, keepdims=True)
    for q in range(n_ia):
        rs[q] = raw_b[q * SUBS : (q + 1) * SUBS]
    rf[a] = rs[a]
    sq_copies = spread(sq.at[mine], sq, mine, peers_all, sq_s, sq_r)
    rf_copies = []
    for step in range(1, n_ia):
        peer = ring_a[step]
        rf_copies.append(
            pltpu.make_async_remote_copy(
                src_ref=rs.at[peer],
                dst_ref=rf.at[a],
                send_sem=rf_s.at[step],
                recv_sem=rf_r.at[step],
                device_id=(peer, j, zero),
                device_id_type=MESH,
            )
        )
    begin(rf_copies)
    begin(sq_copies)
    arrived(rf_copies)
    arrived(sq_copies)
    squares_b = functools.reduce(jnp.add, [sq[s] for s in range(n_all)])
    total_b = jnp.sum(jnp.where(lane == sub, squares_b, 0.0), axis=1, keepdims=True)
    scale_b = jnp.broadcast_to(1.0 / jnp.sqrt(total_b / total_j + EPS), (rank, LANES))
    for q in range(n_ia):
        wsc[q] = scale_b[q * SUBS : (q + 1) * SUBS]
    own = wsc[a]
    for q in range(n_ia):
        ob_ref[:, q * piece_j : (q + 1) * piece_j] = rf[q] * own

    for copy in sends:
        copy.wait_send()


def write_out(a_ref, b_ref, oa_ref, ob_ref, sems):
    copies = [
        pltpu.make_async_copy(a_ref, oa_ref, sems.at[0]),
        pltpu.make_async_copy(b_ref, ob_ref, sems.at[1]),
    ]
    for copy in copies:
        copy.start()
    for copy in copies:
        copy.wait()


def fused(tensor, factor_b, factor_c):
    n_ia = lax.axis_size("ia")
    n_ja = lax.axis_size("ja")
    steps, width_i, width_j = tensor.shape
    rows_b = factor_b.shape[0]
    rank = rows_b * n_ia
    halves = n_ja // (rank // SUBS)
    f32 = jnp.float32
    vmem = pltpu.VMEM
    dma = pltpu.SemaphoreType.DMA
    ja_sems = [dma((n_ja,)), dma((n_ja,))]
    ia_sems = [dma((n_ia,)), dma((n_ia,))]
    all_sems = [dma((n_ia * n_ja,)), dma((n_ia * n_ja,))]
    scratch = [
        vmem(tensor.shape, tensor.dtype),
        vmem((n_ia, rows_b, width_j), f32),
        vmem(factor_c.shape, f32),
        vmem((n_ia * n_ja, 1, LANES), f32),
        vmem((n_ja, SUBS, LANES), f32),
        vmem((n_ja, SUBS, width_i // halves), f32),
        vmem((n_ja, SUBS, width_i // halves), f32),
        vmem((n_ja, SUBS, width_i // halves), f32),
        vmem((rank, width_i), f32),
        vmem((n_ia, SUBS, LANES), f32),
        vmem((n_ia, rank, width_j // n_ia), f32),
        vmem((n_ia, rank, width_j // n_ia), f32),
        vmem((n_ia, SUBS, LANES), f32),
        vmem((n_ia * n_ja, 1, LANES), f32),
        vmem((n_ia, SUBS, width_j // n_ia), f32),
        vmem((n_ia, SUBS, width_j // n_ia), f32),
        vmem((steps, width_i // halves, LANES), f32),
        dma((halves,)),
        dma((2,)),
        *ia_sems, *all_sems, *ja_sems, *ja_sems, *ja_sems, *ia_sems, *ia_sems, *all_sems, *ia_sems,
    ]
    flops = 8 * rank * tensor.size
    results = pl.pallas_call(
        functools.partial(kernel, n_ia, n_ja, width_i * n_ia, width_j * n_ja),
        out_shape=(
            jax.ShapeDtypeStruct((rank // n_ja, width_i), f32),
            jax.ShapeDtypeStruct((rows_b, width_j), f32),
        ),
        in_specs=[
            pl.BlockSpec(memory_space=pltpu.HBM),
            pl.BlockSpec(memory_space=pltpu.HBM),
            pl.BlockSpec(memory_space=pltpu.HBM),
        ],
        out_specs=(pl.BlockSpec(memory_space=pltpu.VMEM), pl.BlockSpec(memory_space=pltpu.VMEM)),
        scratch_shapes=scratch,
        cost_estimate=pl.CostEstimate(flops=flops, bytes_accessed=2 * tensor.size, transcendentals=0),
        compiler_params=pltpu.CompilerParams(
            collective_id=0, has_side_effects=True, vmem_limit_bytes=56 * 2**20
        ),
    )(tensor, factor_b, factor_c)
    anywhere = pl.BlockSpec(memory_space=pl.ANY)
    return pl.pallas_call(
        write_out,
        out_shape=tuple(jax.ShapeDtypeStruct(r.shape, r.dtype) for r in results),
        in_specs=[anywhere, anywhere],
        out_specs=(anywhere, anywhere),
        scratch_shapes=[dma((2,))],
        compiler_params=pltpu.CompilerParams(vmem_limit_bytes=56 * 2**20),
    )(*results)


def fits(mesh):
    n_ia, n_ja, n_ka = (mesh.shape[name] for name in ("ia", "ja", "ka"))
    return n_ka == 1 and n_ia * SUBS == 32 and n_ja == 2 * n_ia


def solution(mesh):
    return jax.shard_map(
        fused if fits(mesh) else body,
        mesh=mesh,
        in_specs=(P("ka", "ia", "ja"), P("ia", ("ja", "ka")), P(("ia", "ja"), "ka")),
        out_specs=(P("ja", ("ia", "ka")), P("ia", ("ja", "ka"))),
        check_vma=False,
    )
```

```python
import functools

import jax
import jax.numpy as jnp
from jax import lax
from jax.experimental import pallas as pl
from jax.experimental.pallas import tpu as pltpu
from jax.sharding import PartitionSpec as P

EPS = 1e-06
HIGH = lax.Precision.HIGHEST


def gram_of(block):
    return jnp.dot(block, block.T, precision=HIGH, preferred_element_type=jnp.float32)


def solve_with(normal, rhs):
    lower = jnp.linalg.cholesky(normal)
    return jax.scipy.linalg.cho_solve((lower, True), rhs)


def arrange(partial_rows, rows_split, cols_split):
    rank, width = partial_rows.shape
    grid = partial_rows.reshape(rows_split, rank // rows_split, cols_split, width // cols_split)
    return grid.transpose(0, 2, 1, 3).reshape(rank * cols_split, width // cols_split)


def assemble(pieces, rows_split, cols_split):
    count, height, width = pieces.shape
    grid = pieces.reshape(rows_split, cols_split, height, width)
    return grid.transpose(0, 2, 1, 3).reshape(rows_split * height, cols_split * width)


def scaled(raw, squares, total):
    return raw / jnp.sqrt(squares / total + EPS)[:, None]


def body(tensor, factor_b, factor_c):
    n_ia = lax.axis_size("ia")
    n_ja = lax.axis_size("ja")
    n_ka = lax.axis_size("ka")
    total_i = tensor.shape[1] * n_ia
    total_j = tensor.shape[2] * n_ja
    c_block = lax.all_gather(factor_c, ("ia", "ja"), axis=0, tiled=True)
    pieces = lax.all_gather(factor_b[None], ("ia", "ka"), axis=0, tiled=True)
    b_block = assemble(pieces, n_ia, n_ka)
    gram_b = lax.psum(gram_of(b_block), "ja")
    gram_c = lax.psum(gram_of(c_block), "ka")
    normal_a = gram_b * gram_c
    kr_a = (c_block[:, :, None] * b_block[:, None, :]).astype(jnp.bfloat16)
    partial_a = jnp.einsum("rkj,kij->ri", kr_a, tensor, preferred_element_type=jnp.float32)
    solved_a = solve_with(normal_a, partial_a)
    raw_a = lax.psum_scatter(
        arrange(solved_a, n_ja, n_ka), ("ja", "ka"), scatter_dimension=0, tiled=True
    )
    squares_a = lax.psum(jnp.sum(raw_a * raw_a, axis=1), ("ia", "ka"))
    local_a = scaled(raw_a, squares_a, total_i)
    pieces_a = lax.all_gather(local_a[None], ("ja", "ka"), axis=0, tiled=True)
    gathered_a = assemble(pieces_a, n_ja, n_ka)
    gram_a = lax.psum(gram_of(gathered_a), "ia")
    normal_b = gram_a * gram_c
    kr_b = (c_block[:, :, None] * gathered_a[:, None, :]).astype(jnp.bfloat16)
    partial_b = jnp.einsum("rki,kij->rj", kr_b, tensor, preferred_element_type=jnp.float32)
    solved_b = solve_with(normal_b, partial_b)
    raw_b = lax.psum_scatter(
        arrange(solved_b, n_ia, n_ka), ("ia", "ka"), scatter_dimension=0, tiled=True
    )
    squares_b = lax.psum(jnp.sum(raw_b * raw_b, axis=1), ("ja", "ka"))
    share_b = scaled(raw_b, squares_b, total_j)
    return (local_a, share_b)


MESH = pl.DeviceIdType.MESH
LANES = 128
SUBS = 8
NT = (((1,), (1,)), ((), ()))


def spread(src, dst, me, peers, send, recv):
    copies = []
    for step, peer in enumerate(peers, 1):
        copies.append(
            pltpu.make_async_remote_copy(
                src_ref=src,
                dst_ref=dst.at[me],
                send_sem=send.at[step],
                recv_sem=recv.at[step],
                device_id=peer,
                device_id_type=MESH,
            )
        )
    return copies


def ring(me, count):
    return [me] + [jnp.where(me + step >= count, me + step - count, me + step) for step in range(1, count)]


def stacked(pieces, rows):
    height, width = sum(p.shape[0] for p in pieces), pieces[0].shape[1]
    if rows > height:
        pieces = list(pieces) + [jnp.zeros((rows - height, width), pieces[0].dtype)]
    return jnp.concatenate(pieces, axis=0)


def wide_gram(block):
    other = stacked([block], LANES)
    return lax.dot_general(block, other, NT, precision=HIGH, preferred_element_type=jnp.float32)


def parts(values, rows):
    high = values.astype(jnp.bfloat16).astype(jnp.float32)
    rest = values - high
    middle = rest.astype(jnp.bfloat16).astype(jnp.float32)
    return stacked([high, middle, rest - middle], rows)


def folded(products, rank):
    total = products[0:rank] + products[rank : 2 * rank] + products[2 * rank : 3 * rank]
    return total + pltpu.roll(total, LANES - rank, 1) + pltpu.roll(total, LANES - 2 * rank, 1)


def masked(gram):
    lane = lax.broadcasted_iota(jnp.int32, gram.shape, 1)
    return jnp.where(lane < gram.shape[0], gram, 0.0)


def applied(solver, values):
    rank = solver.shape[0]
    s_parts = parts(solver, 3 * rank)
    high, middle, low = (s_parts[p * rank : (p + 1) * rank] for p in range(3))
    left = jnp.concatenate(
        [
            high + pltpu.roll(high, rank, 1) + pltpu.roll(high, 2 * rank, 1) + pltpu.roll(middle, 3 * rank, 1),
            middle + pltpu.roll(low, rank, 1),
        ],
        axis=1,
    ).astype(jnp.bfloat16)
    v_high, v_middle, v_low = (
        p.astype(jnp.bfloat16) for p in jnp.split(parts(values, 3 * rank), 3, axis=0)
    )
    blank = jnp.zeros_like(v_high)
    right = jnp.concatenate(
        [v_high, v_middle, v_low, v_high, v_middle, v_high, blank, blank], axis=0
    )
    return jnp.dot(left, right, preferred_element_type=jnp.float32)


def packed(gram):
    rank = gram.shape[0]
    tile = gram[0:SUBS]
    for q in range(1, rank // SUBS):
        tile = tile + pltpu.roll(gram[q * SUBS : (q + 1) * SUBS], q * rank, 1)
    return tile


def unpacked(tile, rank):
    lane = lax.broadcasted_iota(jnp.int32, (SUBS, LANES), 1)
    groups = []
    for q in range(rank // SUBS):
        moved = tile if q == 0 else pltpu.roll(tile, LANES - q * rank, 1)
        groups.append(jnp.where(lane < rank, moved, 0.0))
    return jnp.concatenate(groups, axis=0)


def reciprocal(value):
    guess = pl.reciprocal(value, approx=True)
    guess = guess * (2.0 - value * guess)
    return guess * (2.0 - value * guess)


def inverse(normal):
    rank = normal.shape[0]
    blocks = [normal[q * SUBS : (q + 1) * SUBS] for q in range(rank // SUBS)]
    lane = lax.broadcasted_iota(jnp.int32, (SUBS, LANES), 1)
    sub = lax.broadcasted_iota(jnp.int32, (SUBS, LANES), 0)

    def column(block, index):
        return jnp.broadcast_to(block[:, index : index + 1], (SUBS, LANES))

    for q in range(rank // SUBS):
        first = q * SUBS
        cols = [[column(block, first + k) for k in range(SUBS)] for block in blocks]
        rows, inner = blocks[q], cols[q]
        for k in range(SUBS):
            col = inner[k]
            pivot = reciprocal(col[k : k + 1])
            row = jnp.where(lane[0:1] == first + k, 1.0, rows[k : k + 1]) * pivot
            rest = jnp.where(lane == first + k, 0.0, rows) - col * row
            rows = jnp.where(sub == k, row, rest)
            for m in range(k + 1, SUBS):
                entry = inner[m][k : k + 1] * pivot
                inner[m] = jnp.where(sub == k, entry, inner[m] - col * entry)
        inside = (lane >= first) & (lane < first + SUBS)
        for p in range(rank // SUBS):
            if p != q:
                total = jnp.where(inside, 0.0, blocks[p])
                for k in range(SUBS):
                    total = total - cols[p][k] * rows[k : k + 1]
                blocks[p] = total
        blocks[q] = rows
    return jnp.concatenate(blocks, axis=0)


def split(values):
    high = values.astype(jnp.bfloat16).astype(jnp.float32)
    return high, values - high


def kernel(
    n_ia, n_ja, total_i, total_j,
    t_ref, b_ref, c_ref, oa_ref, ob_ref,
    tv, ball, cin, cs, gb, pbuf, ra, ga, araw, gr, pb, rb, wsc, sq, rs, rf, prod,
    t_sem, in_sem, b_s, b_r, c_s, c_r, gb_s, gb_r, ra_s, ra_r, ga_s, ga_r,
    gr_s, gr_r, rb_s, rb_r, sq_s, sq_r, rf_s, rf_r,
):
    a = lax.axis_index("ia")
    j = lax.axis_index("ja")
    steps, width_i, width_j = tv.shape
    rank = n_ia * b_ref.shape[0]
    groups = rank // SUBS
    halves = n_ja // groups
    part_i = width_i // halves
    cuts_j = 2
    part_j = width_j // cuts_j
    piece_j = width_j // n_ia

    n_all = n_ia * n_ja
    mine = a * n_ja + j

    ring_a, ring_j = ring(a, n_ia), ring(j, n_ja)
    zero = jnp.int32(0)
    peers_ia = [(p, j, zero) for p in ring_a[1:]]
    peers_ja = [(a, q, zero) for q in ring_j[1:]]
    peers_all = [(p, q, zero) for q in reversed(ring_j) for p in ring_a][:-n_ia]
    peers_all = peers_all + peers_ia

    fetch_c = pltpu.make_async_copy(c_ref, cin, in_sem.at[0])
    fetch_b = pltpu.make_async_copy(b_ref, ball.at[a], in_sem.at[1])
    fetch_c.start()
    fetch_b.start()
    loads = []
    for h in range(halves):
        rows = pl.ds(h * part_i, part_i)
        load = pltpu.make_async_copy(t_ref.at[:, rows], tv.at[:, rows], t_sem.at[h])
        load.start()
        loads.append(load)

    barrier = pltpu.get_barrier_semaphore()
    for peer in peers_all:
        pl.semaphore_signal(barrier, inc=1, device_id=peer, device_id_type=MESH)
    fetch_c.wait()
    cs[mine] = jnp.zeros((1, LANES), jnp.float32)
    cs[mine, :, 0:steps] = cin[...]
    fetch_b.wait()
    pl.semaphore_wait(barrier, n_all - 1)

    sends = []

    def begin(copies):
        for copy in copies:
            copy.start()
        sends.extend(copies)
        return copies

    def arrived(copies):
        for copy in copies:
            copy.wait_recv()

    b_copies = begin(spread(ball.at[a], ball, a, peers_ia, b_s, b_r))
    c_copies = begin(spread(cs.at[mine], cs, mine, peers_all, c_s, c_r))
    arrived(b_copies)
    b_parts = parts(stacked([ball[s] for s in range(n_ia)], rank), LANES)
    weights = b_parts.T.astype(jnp.bfloat16)

    ra_copies = []
    for step in range(1, n_ja):
        peer = ring_j[step]
        ra_copies.append(
            pltpu.make_async_remote_copy(
                src_ref=pbuf.at[peer],
                dst_ref=ra.at[j],
                send_sem=ra_s.at[step],
                recv_sem=ra_r.at[step],
                device_id=(a, peer, zero),
                device_id_type=MESH,
            )
        )

    def product_a(h, k):
        return jnp.dot(
            tv[k, h * part_i : (h + 1) * part_i, :], weights, preferred_element_type=jnp.float32
        )

    loads[0].wait()
    for k in range(steps):
        prod[k] = product_a(0, k)
    gb[j] = packed(
        masked(
            folded(
                jnp.dot(b_parts.astype(jnp.bfloat16), weights, preferred_element_type=jnp.float32),
                rank,
            )
        )
    )
    gb_copies = begin(spread(gb.at[j], gb, j, peers_ja, gb_s, gb_r))
    arrived(c_copies)
    c_all = stacked([cs[s] for s in range(n_all)], rank)
    c_rows = stacked([c_all, c_all, c_all], LANES).T
    for h in range(halves):
        if h:
            loads[h].wait()
        total = jnp.zeros((part_i, LANES), jnp.float32)
        for k in range(steps):
            product = product_a(h, k) if h else prod[k]
            total = total + product * c_rows[k : k + 1, :]
        total = total.T
        total = total[0:rank] + total[rank : 2 * rank] + total[2 * rank : 3 * rank]
        for q in range(groups):
            pbuf[q * halves + h] = total[q * SUBS : (q + 1) * SUBS]
        for step in range(1, n_ja):
            @pl.when(lax.rem(ring_j[step], halves) == h)
            def _():
                ra_copies[step - 1].start()
    sends.extend(ra_copies)
    ra[j] = pbuf[j]
    gram_c = wide_gram(c_all)

    arrived(ra_copies)
    ga[j] = functools.reduce(jnp.add, [ra[s] for s in range(n_ja)])
    ga_copies = begin(spread(ga.at[j], ga, j, peers_ja, ga_s, ga_r))
    c_cols = [c_all[:, k : k + 1] for k in range(steps)]
    arrived(gb_copies)
    gram_b = unpacked(functools.reduce(jnp.add, [gb[s] for s in range(n_ja)]), rank)
    solve_a = inverse(gram_b * gram_c)
    arrived(ga_copies)
    summed = stacked(
        [
            jnp.concatenate([ga[q * halves + h] for h in range(halves)], axis=1)
            for q in range(groups)
        ],
        rank,
    )
    raw_a = applied(solve_a, summed)
    araw[...] = raw_a
    a_parts = parts(raw_a, LANES).astype(jnp.bfloat16)
    products = lax.dot_general(a_parts, a_parts, NT, preferred_element_type=jnp.float32)
    gr[a] = packed(masked(folded(products, rank)))
    gr_copies = begin(spread(gr.at[a], gr, a, peers_ia, gr_s, gr_r))

    rb_copies = []
    for step in range(1, n_ia):
        peer = ring_a[step]
        rb_copies.append(
            pltpu.make_async_remote_copy(
                src_ref=pb.at[peer],
                dst_ref=rb.at[a],
                send_sem=rb_s.at[step],
                recv_sem=rb_r.at[step],
                device_id=(peer, j, zero),
                device_id_type=MESH,
            )
        )
    pieces = []
    for k in range(steps):
        pieces.append(jnp.concatenate(split(raw_a * c_cols[k]), axis=0).astype(jnp.bfloat16))
    for h in range(cuts_j):
        if h:
            arrived(gr_copies)
            gram_a = unpacked(functools.reduce(jnp.add, [gr[s] for s in range(n_ia)]), rank)
            lane = lax.broadcasted_iota(jnp.int32, (rank, LANES), 1)
            sub = lax.broadcasted_iota(jnp.int32, (rank, LANES), 0)
            squares = jnp.where(lane == sub, gram_a, 0.0)
            scale_col = 1.0 / jnp.sqrt(jnp.sum(squares, axis=1, keepdims=True) / total_i + EPS)
            scale_row = 1.0 / jnp.sqrt(jnp.sum(squares, axis=0, keepdims=True) / total_i + EPS)
            solve_b = inverse(gram_a * scale_col * scale_row * gram_c) * scale_row
        total = jnp.zeros((2 * rank, part_j), jnp.float32)
        for k in range(steps):
            total = total + jnp.dot(
                pieces[k], tv[k, :, h * part_j : (h + 1) * part_j], preferred_element_type=jnp.float32
            )
        total = total[0:rank] + total[rank : 2 * rank]
        for m in range(n_ia // cuts_j):
            pb[h * (n_ia // cuts_j) + m] = total[:, m * piece_j : (m + 1) * piece_j]
    begin(rb_copies)
    rb[a] = pb[a]
    new_a = araw[...] * scale_col
    for q in range(groups):
        araw[q * SUBS : (q + 1) * SUBS] = new_a[q * SUBS : (q + 1) * SUBS]
    height = rank // n_ja
    for p in range(n_ja):
        @pl.when(j == p)
        def _():
            oa_ref[...] = araw[p * height : (p + 1) * height, :]

    arrived(rb_copies)
    summed_b = functools.reduce(jnp.add, [rb[s] for s in range(n_ia)])
    raw_b = applied(solve_b, summed_b)
    sums = jnp.sum(raw_b * raw_b, axis=1, keepdims=True)
    sq[mine] = jnp.sum(jnp.where(lane == sub, sums, 0.0), axis=0, keepdims=True)
    for q in range(n_ia):
        rs[q] = raw_b[q * SUBS : (q + 1) * SUBS]
    rf[a] = rs[a]
    sq_copies = spread(sq.at[mine], sq, mine, peers_all, sq_s, sq_r)
    rf_copies = []
    for step in range(1, n_ia):
        peer = ring_a[step]
        rf_copies.append(
            pltpu.make_async_remote_copy(
                src_ref=rs.at[peer],
                dst_ref=rf.at[a],
                send_sem=rf_s.at[step],
                recv_sem=rf_r.at[step],
                device_id=(peer, j, zero),
                device_id_type=MESH,
            )
        )
    begin(rf_copies)
    begin(sq_copies)
    arrived(rf_copies)
    arrived(sq_copies)
    squares_b = functools.reduce(jnp.add, [sq[s] for s in range(n_all)])
    total_b = jnp.sum(jnp.where(lane == sub, squares_b, 0.0), axis=1, keepdims=True)
    scale_b = jnp.broadcast_to(1.0 / jnp.sqrt(total_b / total_j + EPS), (rank, LANES))
    for q in range(n_ia):
        wsc[q] = scale_b[q * SUBS : (q + 1) * SUBS]
    own = wsc[a]
    for q in range(n_ia):
        ob_ref[:, q * piece_j : (q + 1) * piece_j] = rf[q] * own

    for copy in sends:
        copy.wait_send()


def write_out(a_ref, b_ref, oa_ref, ob_ref, sems):
    copies = [
        pltpu.make_async_copy(a_ref, oa_ref, sems.at[0]),
        pltpu.make_async_copy(b_ref, ob_ref, sems.at[1]),
    ]
    for copy in copies:
        copy.start()
    for copy in copies:
        copy.wait()


def fused(tensor, factor_b, factor_c):
    n_ia = lax.axis_size("ia")
    n_ja = lax.axis_size("ja")
    steps, width_i, width_j = tensor.shape
    rows_b = factor_b.shape[0]
    rank = rows_b * n_ia
    halves = n_ja // (rank // SUBS)
    f32 = jnp.float32
    vmem = pltpu.VMEM
    dma = pltpu.SemaphoreType.DMA
    ja_sems = [dma((n_ja,)), dma((n_ja,))]
    ia_sems = [dma((n_ia,)), dma((n_ia,))]
    all_sems = [dma((n_ia * n_ja,)), dma((n_ia * n_ja,))]
    scratch = [
        vmem(tensor.shape, tensor.dtype),
        vmem((n_ia, rows_b, width_j), f32),
        vmem(factor_c.shape, f32),
        vmem((n_ia * n_ja, 1, LANES), f32),
        vmem((n_ja, SUBS, LANES), f32),
        vmem((n_ja, SUBS, width_i // halves), f32),
        vmem((n_ja, SUBS, width_i // halves), f32),
        vmem((n_ja, SUBS, width_i // halves), f32),
        vmem((rank, width_i), f32),
        vmem((n_ia, SUBS, LANES), f32),
        vmem((n_ia, rank, width_j // n_ia), f32),
        vmem((n_ia, rank, width_j // n_ia), f32),
        vmem((n_ia, SUBS, LANES), f32),
        vmem((n_ia * n_ja, 1, LANES), f32),
        vmem((n_ia, SUBS, width_j // n_ia), f32),
        vmem((n_ia, SUBS, width_j // n_ia), f32),
        vmem((steps, width_i // halves, LANES), f32),
        dma((halves,)),
        dma((2,)),
        *ia_sems, *all_sems, *ja_sems, *ja_sems, *ja_sems, *ia_sems, *ia_sems, *all_sems, *ia_sems,
    ]
    flops = 8 * rank * tensor.size
    results = pl.pallas_call(
        functools.partial(kernel, n_ia, n_ja, width_i * n_ia, width_j * n_ja),
        out_shape=(
            jax.ShapeDtypeStruct((rank // n_ja, width_i), f32),
            jax.ShapeDtypeStruct((rows_b, width_j), f32),
        ),
        in_specs=[
            pl.BlockSpec(memory_space=pltpu.HBM),
            pl.BlockSpec(memory_space=pltpu.HBM),
            pl.BlockSpec(memory_space=pltpu.HBM),
        ],
        out_specs=(pl.BlockSpec(memory_space=pltpu.VMEM), pl.BlockSpec(memory_space=pltpu.VMEM)),
        scratch_shapes=scratch,
        cost_estimate=pl.CostEstimate(flops=flops, bytes_accessed=2 * tensor.size, transcendentals=0),
        compiler_params=pltpu.CompilerParams(
            collective_id=0, has_side_effects=True, vmem_limit_bytes=56 * 2**20
        ),
    )(tensor, factor_b, factor_c)
    anywhere = pl.BlockSpec(memory_space=pl.ANY)
    return pl.pallas_call(
        write_out,
        out_shape=tuple(jax.ShapeDtypeStruct(r.shape, r.dtype) for r in results),
        in_specs=[anywhere, anywhere],
        out_specs=(anywhere, anywhere),
        scratch_shapes=[dma((2,))],
        compiler_params=pltpu.CompilerParams(vmem_limit_bytes=56 * 2**20),
    )(*results)


def fits(mesh):
    n_ia, n_ja, n_ka = (mesh.shape[name] for name in ("ia", "ja", "ka"))
    return n_ka == 1 and n_ia * SUBS == 32 and n_ja == 2 * n_ia


def solution(mesh):
    return jax.shard_map(
        fused if fits(mesh) else body,
        mesh=mesh,
        in_specs=(P("ka", "ia", "ja"), P("ia", ("ja", "ka")), P(("ia", "ja"), "ka")),
        out_specs=(P("ja", ("ia", "ka")), P("ia", ("ja", "ka"))),
        check_vma=False,
    )
```

```python
import functools

import jax
import jax.numpy as jnp
from jax import lax
from jax.experimental import pallas as pl
from jax.experimental.pallas import tpu as pltpu
from jax.sharding import PartitionSpec as P

EPS = 1e-06
HIGH = lax.Precision.HIGHEST


def gram_of(block):
    return jnp.dot(block, block.T, precision=HIGH, preferred_element_type=jnp.float32)


def solve_with(normal, rhs):
    lower = jnp.linalg.cholesky(normal)
    return jax.scipy.linalg.cho_solve((lower, True), rhs)


def arrange(partial_rows, rows_split, cols_split):
    rank, width = partial_rows.shape
    grid = partial_rows.reshape(rows_split, rank // rows_split, cols_split, width // cols_split)
    return grid.transpose(0, 2, 1, 3).reshape(rank * cols_split, width // cols_split)


def assemble(pieces, rows_split, cols_split):
    count, height, width = pieces.shape
    grid = pieces.reshape(rows_split, cols_split, height, width)
    return grid.transpose(0, 2, 1, 3).reshape(rows_split * height, cols_split * width)


def scaled(raw, squares, total):
    return raw / jnp.sqrt(squares / total + EPS)[:, None]


def body(tensor, factor_b, factor_c):
    n_ia = lax.axis_size("ia")
    n_ja = lax.axis_size("ja")
    n_ka = lax.axis_size("ka")
    total_i = tensor.shape[1] * n_ia
    total_j = tensor.shape[2] * n_ja
    c_block = lax.all_gather(factor_c, ("ia", "ja"), axis=0, tiled=True)
    pieces = lax.all_gather(factor_b[None], ("ia", "ka"), axis=0, tiled=True)
    b_block = assemble(pieces, n_ia, n_ka)
    gram_b = lax.psum(gram_of(b_block), "ja")
    gram_c = lax.psum(gram_of(c_block), "ka")
    normal_a = gram_b * gram_c
    kr_a = (c_block[:, :, None] * b_block[:, None, :]).astype(jnp.bfloat16)
    partial_a = jnp.einsum("rkj,kij->ri", kr_a, tensor, preferred_element_type=jnp.float32)
    solved_a = solve_with(normal_a, partial_a)
    raw_a = lax.psum_scatter(
        arrange(solved_a, n_ja, n_ka), ("ja", "ka"), scatter_dimension=0, tiled=True
    )
    squares_a = lax.psum(jnp.sum(raw_a * raw_a, axis=1), ("ia", "ka"))
    local_a = scaled(raw_a, squares_a, total_i)
    pieces_a = lax.all_gather(local_a[None], ("ja", "ka"), axis=0, tiled=True)
    gathered_a = assemble(pieces_a, n_ja, n_ka)
    gram_a = lax.psum(gram_of(gathered_a), "ia")
    normal_b = gram_a * gram_c
    kr_b = (c_block[:, :, None] * gathered_a[:, None, :]).astype(jnp.bfloat16)
    partial_b = jnp.einsum("rki,kij->rj", kr_b, tensor, preferred_element_type=jnp.float32)
    solved_b = solve_with(normal_b, partial_b)
    raw_b = lax.psum_scatter(
        arrange(solved_b, n_ia, n_ka), ("ia", "ka"), scatter_dimension=0, tiled=True
    )
    squares_b = lax.psum(jnp.sum(raw_b * raw_b, axis=1), ("ja", "ka"))
    share_b = scaled(raw_b, squares_b, total_j)
    return (local_a, share_b)


MESH = pl.DeviceIdType.MESH
LANES = 128
SUBS = 8
NT = (((1,), (1,)), ((), ()))


def spread(src, dst, me, peers, send, recv):
    copies = []
    for step, peer in enumerate(peers, 1):
        copies.append(
            pltpu.make_async_remote_copy(
                src_ref=src,
                dst_ref=dst.at[me],
                send_sem=send.at[step],
                recv_sem=recv.at[step],
                device_id=peer,
                device_id_type=MESH,
            )
        )
    return copies


def ring(me, count):
    return [me] + [jnp.where(me + step >= count, me + step - count, me + step) for step in range(1, count)]


def stacked(pieces, rows):
    height, width = sum(p.shape[0] for p in pieces), pieces[0].shape[1]
    if rows > height:
        pieces = list(pieces) + [jnp.zeros((rows - height, width), pieces[0].dtype)]
    return jnp.concatenate(pieces, axis=0)


def wide_gram(block):
    other = stacked([block], LANES)
    return lax.dot_general(block, other, NT, precision=HIGH, preferred_element_type=jnp.float32)


def parts(values, rows):
    high = values.astype(jnp.bfloat16).astype(jnp.float32)
    rest = values - high
    middle = rest.astype(jnp.bfloat16).astype(jnp.float32)
    return stacked([high, middle, rest - middle], rows)


def folded(products, rank):
    total = products[0:rank] + products[rank : 2 * rank] + products[2 * rank : 3 * rank]
    return total + pltpu.roll(total, LANES - rank, 1) + pltpu.roll(total, LANES - 2 * rank, 1)


def masked(gram):
    lane = lax.broadcasted_iota(jnp.int32, gram.shape, 1)
    return jnp.where(lane < gram.shape[0], gram, 0.0)


def applied(solver, values):
    rank = solver.shape[0]
    s_parts = parts(solver, 3 * rank)
    high, middle, low = (s_parts[p * rank : (p + 1) * rank] for p in range(3))
    left = jnp.concatenate(
        [
            high + pltpu.roll(high, rank, 1) + pltpu.roll(high, 2 * rank, 1) + pltpu.roll(middle, 3 * rank, 1),
            middle + pltpu.roll(low, rank, 1),
        ],
        axis=1,
    ).astype(jnp.bfloat16)
    v_high, v_middle, v_low = (
        p.astype(jnp.bfloat16) for p in jnp.split(parts(values, 3 * rank), 3, axis=0)
    )
    blank = jnp.zeros_like(v_high)
    right = jnp.concatenate(
        [v_high, v_middle, v_low, v_high, v_middle, v_high, blank, blank], axis=0
    )
    return jnp.dot(left, right, preferred_element_type=jnp.float32)


def packed(gram):
    rank = gram.shape[0]
    tile = gram[0:SUBS]
    for q in range(1, rank // SUBS):
        tile = tile + pltpu.roll(gram[q * SUBS : (q + 1) * SUBS], q * rank, 1)
    return tile


def unpacked(tile, rank):
    lane = lax.broadcasted_iota(jnp.int32, (SUBS, LANES), 1)
    groups = []
    for q in range(rank // SUBS):
        moved = tile if q == 0 else pltpu.roll(tile, LANES - q * rank, 1)
        groups.append(jnp.where(lane < rank, moved, 0.0))
    return jnp.concatenate(groups, axis=0)


def reciprocal(value):
    guess = pl.reciprocal(value, approx=True)
    guess = guess * (2.0 - value * guess)
    return guess * (2.0 - value * guess)


def inverse(normal):
    rank = normal.shape[0]
    blocks = [normal[q * SUBS : (q + 1) * SUBS] for q in range(rank // SUBS)]
    lane = lax.broadcasted_iota(jnp.int32, (SUBS, LANES), 1)
    sub = lax.broadcasted_iota(jnp.int32, (SUBS, LANES), 0)

    def column(block, index):
        return jnp.broadcast_to(block[:, index : index + 1], (SUBS, LANES))

    for q in range(rank // SUBS):
        first = q * SUBS
        cols = [[column(block, first + k) for k in range(SUBS)] for block in blocks]
        rows, inner = blocks[q], cols[q]
        for k in range(SUBS):
            col = inner[k]
            pivot = reciprocal(col[k : k + 1])
            row = jnp.where(lane[0:1] == first + k, 1.0, rows[k : k + 1]) * pivot
            rest = jnp.where(lane == first + k, 0.0, rows) - col * row
            rows = jnp.where(sub == k, row, rest)
            for m in range(k + 1, SUBS):
                entry = inner[m][k : k + 1] * pivot
                inner[m] = jnp.where(sub == k, entry, inner[m] - col * entry)
        inside = (lane >= first) & (lane < first + SUBS)
        for p in range(rank // SUBS):
            if p != q:
                total = jnp.where(inside, 0.0, blocks[p])
                for k in range(SUBS):
                    total = total - cols[p][k] * rows[k : k + 1]
                blocks[p] = total
        blocks[q] = rows
    return jnp.concatenate(blocks, axis=0)


def split(values):
    high = values.astype(jnp.bfloat16).astype(jnp.float32)
    return high, values - high


def kernel(
    n_ia, n_ja, total_i, total_j,
    t_ref, b_ref, c_ref, oa_ref, ob_ref,
    tv, ball, cin, cs, gb, pbuf, ra, ga, araw, gr, pb, rb, wsc, sq, rs, rf, prod,
    t_sem, in_sem, b_s, b_r, c_s, c_r, gb_s, gb_r, ra_s, ra_r, ga_s, ga_r,
    gr_s, gr_r, rb_s, rb_r, sq_s, sq_r, rf_s, rf_r,
):
    a = lax.axis_index("ia")
    j = lax.axis_index("ja")
    steps, width_i, width_j = tv.shape
    rank = n_ia * b_ref.shape[0]
    groups = rank // SUBS
    halves = n_ja // groups
    part_i = width_i // halves
    cuts_j = 2
    part_j = width_j // cuts_j
    piece_j = width_j // n_ia

    n_all = n_ia * n_ja
    mine = a * n_ja + j

    ring_a, ring_j = ring(a, n_ia), ring(j, n_ja)
    zero = jnp.int32(0)
    peers_ia = [(p, j, zero) for p in ring_a[1:]]
    peers_ja = [(a, q, zero) for q in ring_j[1:]]
    peers_all = [(p, q, zero) for q in reversed(ring_j) for p in ring_a][:-n_ia]
    peers_all = peers_all + peers_ia

    fetch_c = pltpu.make_async_copy(c_ref, cin, in_sem.at[0])
    fetch_b = pltpu.make_async_copy(b_ref, ball.at[a], in_sem.at[1])
    fetch_c.start()
    fetch_b.start()
    loads = []
    for h in range(halves):
        rows = pl.ds(h * part_i, part_i)
        load = pltpu.make_async_copy(t_ref.at[:, rows], tv.at[:, rows], t_sem.at[h])
        load.start()
        loads.append(load)

    barrier = pltpu.get_barrier_semaphore()
    for peer in peers_all:
        pl.semaphore_signal(barrier, inc=1, device_id=peer, device_id_type=MESH)
    fetch_c.wait()
    cs[mine] = jnp.zeros((1, LANES), jnp.float32)
    cs[mine, :, 0:steps] = cin[...]
    fetch_b.wait()
    pl.semaphore_wait(barrier, n_all - 1)

    sends = []

    def begin(copies):
        for copy in copies:
            copy.start()
        sends.extend(copies)
        return copies

    def arrived(copies):
        for copy in copies:
            copy.wait_recv()

    b_copies = begin(spread(ball.at[a], ball, a, peers_ia, b_s, b_r))
    c_copies = begin(spread(cs.at[mine], cs, mine, peers_all, c_s, c_r))
    arrived(b_copies)
    b_parts = parts(stacked([ball[s] for s in range(n_ia)], rank), LANES)
    weights = b_parts.T.astype(jnp.bfloat16)

    ra_copies = []
    for step in range(1, n_ja):
        peer = ring_j[step]
        ra_copies.append(
            pltpu.make_async_remote_copy(
                src_ref=pbuf.at[peer],
                dst_ref=ra.at[j],
                send_sem=ra_s.at[step],
                recv_sem=ra_r.at[step],
                device_id=(a, peer, zero),
                device_id_type=MESH,
            )
        )

    def product_a(h, k):
        return jnp.dot(
            tv[k, h * part_i : (h + 1) * part_i, :], weights, preferred_element_type=jnp.float32
        )

    loads[0].wait()
    for k in range(steps):
        prod[k] = product_a(0, k)
    gb[j] = packed(
        masked(
            folded(
                jnp.dot(b_parts.astype(jnp.bfloat16), weights, preferred_element_type=jnp.float32),
                rank,
            )
        )
    )
    gb_copies = begin(spread(gb.at[j], gb, j, peers_ja, gb_s, gb_r))
    arrived(c_copies)
    c_all = stacked([cs[s] for s in range(n_all)], rank)
    c_rows = stacked([c_all, c_all, c_all], LANES).T
    for h in range(halves):
        if h:
            loads[h].wait()
        total = jnp.zeros((part_i, LANES), jnp.float32)
        for k in range(steps):
            product = product_a(h, k) if h else prod[k]
            total = total + product * c_rows[k : k + 1, :]
        total = total.T
        total = total[0:rank] + total[rank : 2 * rank] + total[2 * rank : 3 * rank]
        for q in range(groups):
            pbuf[q * halves + h] = total[q * SUBS : (q + 1) * SUBS]
        for step in range(1, n_ja):
            @pl.when(lax.rem(ring_j[step], halves) == h)
            def _():
                ra_copies[step - 1].start()
    sends.extend(ra_copies)
    ra[j] = pbuf[j]
    gram_c = wide_gram(c_all)

    arrived(ra_copies)
    ga[j] = functools.reduce(jnp.add, [ra[s] for s in range(n_ja)])
    ga_copies = begin(spread(ga.at[j], ga, j, peers_ja, ga_s, ga_r))
    c_cols = [c_all[:, k : k + 1] for k in range(steps)]
    arrived(gb_copies)
    gram_b = unpacked(functools.reduce(jnp.add, [gb[s] for s in range(n_ja)]), rank)
    solve_a = inverse(gram_b * gram_c)
    arrived(ga_copies)
    summed = stacked(
        [
            jnp.concatenate([ga[q * halves + h] for h in range(halves)], axis=1)
            for q in range(groups)
        ],
        rank,
    )
    raw_a = applied(solve_a, summed)
    araw[...] = raw_a
    a_parts = parts(raw_a, LANES).astype(jnp.bfloat16)
    products = lax.dot_general(a_parts, a_parts, NT, preferred_element_type=jnp.float32)
    gr[a] = packed(masked(folded(products, rank)))
    gr_copies = begin(spread(gr.at[a], gr, a, peers_ia, gr_s, gr_r))

    rb_copies = []
    for step in range(1, n_ia):
        peer = ring_a[step]
        rb_copies.append(
            pltpu.make_async_remote_copy(
                src_ref=pb.at[peer],
                dst_ref=rb.at[a],
                send_sem=rb_s.at[step],
                recv_sem=rb_r.at[step],
                device_id=(peer, j, zero),
                device_id_type=MESH,
            )
        )
    pieces = []
    for k in range(steps):
        pieces.append(jnp.concatenate(split(raw_a * c_cols[k]), axis=0).astype(jnp.bfloat16))
    for h in range(cuts_j):
        total = jnp.zeros((2 * rank, part_j), jnp.float32)
        for k in range(steps):
            total = total + jnp.dot(
                pieces[k], tv[k, :, h * part_j : (h + 1) * part_j], preferred_element_type=jnp.float32
            )
        total = total[0:rank] + total[rank : 2 * rank]
        for m in range(n_ia // cuts_j):
            pb[h * (n_ia // cuts_j) + m] = total[:, m * piece_j : (m + 1) * piece_j]
        for step in range(1, n_ia):
            @pl.when(ring_a[step] // (n_ia // cuts_j) == h)
            def _():
                rb_copies[step - 1].start()
    sends.extend(rb_copies)
    rb[a] = pb[a]

    arrived(gr_copies)
    gram_a = unpacked(functools.reduce(jnp.add, [gr[s] for s in range(n_ia)]), rank)
    lane = lax.broadcasted_iota(jnp.int32, (rank, LANES), 1)
    sub = lax.broadcasted_iota(jnp.int32, (rank, LANES), 0)
    squares = jnp.where(lane == sub, gram_a, 0.0)
    scale_col = 1.0 / jnp.sqrt(jnp.sum(squares, axis=1, keepdims=True) / total_i + EPS)
    scale_row = 1.0 / jnp.sqrt(jnp.sum(squares, axis=0, keepdims=True) / total_i + EPS)
    solve_b = inverse(gram_a * scale_col * scale_row * gram_c) * scale_row
    new_a = araw[...] * scale_col
    for q in range(groups):
        araw[q * SUBS : (q + 1) * SUBS] = new_a[q * SUBS : (q + 1) * SUBS]
    height = rank // n_ja
    for p in range(n_ja):
        @pl.when(j == p)
        def _():
            oa_ref[...] = araw[p * height : (p + 1) * height, :]

    arrived(rb_copies)
    summed_b = functools.reduce(jnp.add, [rb[s] for s in range(n_ia)])
    raw_b = applied(solve_b, summed_b)
    sums = jnp.sum(raw_b * raw_b, axis=1, keepdims=True)
    sq[mine] = jnp.sum(jnp.where(lane == sub, sums, 0.0), axis=0, keepdims=True)
    for q in range(n_ia):
        rs[q] = raw_b[q * SUBS : (q + 1) * SUBS]
    rf[a] = rs[a]
    sq_copies = spread(sq.at[mine], sq, mine, peers_all, sq_s, sq_r)
    rf_copies = []
    for step in range(1, n_ia):
        peer = ring_a[step]
        rf_copies.append(
            pltpu.make_async_remote_copy(
                src_ref=rs.at[peer],
                dst_ref=rf.at[a],
                send_sem=rf_s.at[step],
                recv_sem=rf_r.at[step],
                device_id=(peer, j, zero),
                device_id_type=MESH,
            )
        )
    begin(rf_copies)
    begin(sq_copies)
    arrived(rf_copies)
    arrived(sq_copies)
    squares_b = functools.reduce(jnp.add, [sq[s] for s in range(n_all)])
    total_b = jnp.sum(jnp.where(lane == sub, squares_b, 0.0), axis=1, keepdims=True)
    scale_b = jnp.broadcast_to(1.0 / jnp.sqrt(total_b / total_j + EPS), (rank, LANES))
    for q in range(n_ia):
        wsc[q] = scale_b[q * SUBS : (q + 1) * SUBS]
    own = wsc[a]
    for q in range(n_ia):
        ob_ref[:, q * piece_j : (q + 1) * piece_j] = rf[q] * own

    for copy in sends:
        copy.wait_send()


def write_out(a_ref, b_ref, oa_ref, ob_ref, sems):
    copies = [
        pltpu.make_async_copy(a_ref, oa_ref, sems.at[0]),
        pltpu.make_async_copy(b_ref, ob_ref, sems.at[1]),
    ]
    for copy in copies:
        copy.start()
    for copy in copies:
        copy.wait()


def fused(tensor, factor_b, factor_c):
    n_ia = lax.axis_size("ia")
    n_ja = lax.axis_size("ja")
    steps, width_i, width_j = tensor.shape
    rows_b = factor_b.shape[0]
    rank = rows_b * n_ia
    halves = n_ja // (rank // SUBS)
    f32 = jnp.float32
    vmem = pltpu.VMEM
    dma = pltpu.SemaphoreType.DMA
    ja_sems = [dma((n_ja,)), dma((n_ja,))]
    ia_sems = [dma((n_ia,)), dma((n_ia,))]
    all_sems = [dma((n_ia * n_ja,)), dma((n_ia * n_ja,))]
    scratch = [
        vmem(tensor.shape, tensor.dtype),
        vmem((n_ia, rows_b, width_j), f32),
        vmem(factor_c.shape, f32),
        vmem((n_ia * n_ja, 1, LANES), f32),
        vmem((n_ja, SUBS, LANES), f32),
        vmem((n_ja, SUBS, width_i // halves), f32),
        vmem((n_ja, SUBS, width_i // halves), f32),
        vmem((n_ja, SUBS, width_i // halves), f32),
        vmem((rank, width_i), f32),
        vmem((n_ia, SUBS, LANES), f32),
        vmem((n_ia, rank, width_j // n_ia), f32),
        vmem((n_ia, rank, width_j // n_ia), f32),
        vmem((n_ia, SUBS, LANES), f32),
        vmem((n_ia * n_ja, 1, LANES), f32),
        vmem((n_ia, SUBS, width_j // n_ia), f32),
        vmem((n_ia, SUBS, width_j // n_ia), f32),
        vmem((steps, width_i // halves, LANES), f32),
        dma((halves,)),
        dma((2,)),
        *ia_sems, *all_sems, *ja_sems, *ja_sems, *ja_sems, *ia_sems, *ia_sems, *all_sems, *ia_sems,
    ]
    flops = 8 * rank * tensor.size
    results = pl.pallas_call(
        functools.partial(kernel, n_ia, n_ja, width_i * n_ia, width_j * n_ja),
        out_shape=(
            jax.ShapeDtypeStruct((rank // n_ja, width_i), f32),
            jax.ShapeDtypeStruct((rows_b, width_j), f32),
        ),
        in_specs=[
            pl.BlockSpec(memory_space=pltpu.HBM),
            pl.BlockSpec(memory_space=pltpu.HBM),
            pl.BlockSpec(memory_space=pltpu.HBM),
        ],
        out_specs=(pl.BlockSpec(memory_space=pltpu.VMEM), pl.BlockSpec(memory_space=pltpu.VMEM)),
        scratch_shapes=scratch,
        cost_estimate=pl.CostEstimate(flops=flops, bytes_accessed=2 * tensor.size, transcendentals=0),
        compiler_params=pltpu.CompilerParams(
            collective_id=0, has_side_effects=True, vmem_limit_bytes=56 * 2**20
        ),
    )(tensor, factor_b, factor_c)
    anywhere = pl.BlockSpec(memory_space=pl.ANY)
    return pl.pallas_call(
        write_out,
        out_shape=tuple(jax.ShapeDtypeStruct(r.shape, r.dtype) for r in results),
        in_specs=[anywhere, anywhere],
        out_specs=(anywhere, anywhere),
        scratch_shapes=[dma((2,))],
        compiler_params=pltpu.CompilerParams(vmem_limit_bytes=56 * 2**20),
    )(*results)


def fits(mesh):
    n_ia, n_ja, n_ka = (mesh.shape[name] for name in ("ia", "ja", "ka"))
    return n_ka == 1 and n_ia * SUBS == 32 and n_ja == 2 * n_ia


def solution(mesh):
    return jax.shard_map(
        fused if fits(mesh) else body,
        mesh=mesh,
        in_specs=(P("ka", "ia", "ja"), P("ia", ("ja", "ka")), P(("ia", "ja"), "ka")),
        out_specs=(P("ja", ("ia", "ka")), P("ia", ("ja", "ka"))),
        check_vma=False,
    )
```
